256 devices in a mesh: dp: 32 (over z, x_hi, core), fsdp: 8 (over x_lo, y).
Axes of the slice: x: 4 (x_hi: 2, x_lo: 2; x = x_hi * 2 + x_lo), y: 4, z: 8, core: 2. Of those that a mesh axis runs over, the one named last changes fastest.
Arguments:
- attn: bfloat16 [147456, 1536], P(('dp', 'fsdp')), may hold values from -6 to 6
- cotangent: bfloat16 [147456, 3072], P(('dp', 'fsdp')), may hold values from -24 to 24
- weight: bfloat16 [1536, 3072], P('fsdp'), may hold values from -0.15625 to 0.15625
- projector: bfloat16 [1536, 256], replicated, may hold values from -0.15625 to 0.15625
- moment_one: float32 [3072, 256], P(('dp', 'fsdp')), may hold values from -256 to 256
- moment_two: float32 [3072, 256], P(('dp', 'fsdp')), may hold values from 30 to 3000
- step_count: int32 [1], replicated, may hold values from 1 to 10
Outputs:
- grad_input: bfloat16 [147456, 1536], P(('dp', 'fsdp'))
- weight_step: float32 [1536, 3072], P('fsdp')
- first_moment: float32 [3072, 256], P(('dp', 'fsdp'))
- second_moment: float32 [3072, 256], P(('dp', 'fsdp'))
The draws below stay inside these ranges and needn't reach their ends.
All inputs are finite; a program needn't handle non-finite values.
Results may differ from the reference program's by a relative error of at most 0.015.
Values may be sent and summed in bfloat16 or wider, within the bound.
A program may use at most 128 MiB of HBM per device.

```python
import math
import jax
import jax.numpy as jnp
from jax import lax

D = 3072
DI = 1536
R = 256
TOKENS = 147456


def raised(array, rng, source, target, blocks, factor):
    def block_of(position):
        return (jnp.arange(array.shape[position]) // (array.shape[position] // blocks)).reshape((-1,) + (1,) * (array.ndim - 1 - position))

    near = jax.random.permutation(rng, blocks)[block_of(target)]
    second = (block_of(target) + blocks // 2) % blocks
    return jnp.where((block_of(source) == near) | (block_of(source) == second), factor * array, array)


def level_of(stream_key, extent, split, smallest, largest):
    loudness = 1.0
    for position, shards_of in split:
        steps = jax.random.uniform(jax.random.fold_in(jax.random.fold_in(stream_key, 6), position), (shards_of,), jnp.float32, smallest / len(split), largest / len(split))
        loudness = loudness * jnp.repeat(jnp.exp(steps), extent[position] // shards_of).reshape((-1,) + (1,) * (len(extent) - 1 - position))
    return loudness


def gaussian(key, shape, spread, limit, split=(), held_as=jnp.bfloat16):
    entries = jax.random.normal(key, shape, jnp.float32) * spread
    if len(split) > 0:
        entries = level_of(key, shape, split, -0.22, 0.18) * entries
    return jnp.clip(entries, min=-limit, max=limit).astype(held_as)


def bell_draw_with(key, extent, width, most, split, heavy, held_as=jnp.bfloat16):
    array = width * jax.random.normal(key, extent, jnp.float32)
    if split:
        array = array * level_of(key, extent, split, -0.22, 0.18)
    return jnp.clip(raised(array, jax.random.fold_in(key, 3), *heavy), -most, most).astype(held_as)


def setup_inputs(seed: int = 0) -> dict:
    splits = jax.random.split(jax.random.key(seed), 8)
    attn = gaussian(splits[0], (TOKENS, DI), 1.0, 6.0, ((0, 256),))
    cotangent = bell_draw_with(splits[1], (TOKENS, D), 1.0, 24.0, ((0, 256),), (0, 1, 256, 6.0))
    weight = gaussian(splits[2], (DI, D), DI ** -0.5, 0.15625, ((0, 8),))
    projector = gaussian(splits[3], (DI, R), DI ** -0.5, 0.15625)
    moment_one = gaussian(splits[4], (D, R), 40.0, 256.0, ((0, 256),), jnp.float32)
    moment_two = jnp.clip(jnp.exp(math.log(3000.0) - 4.6051702 * jax.random.uniform(splits[5], (D, R), jnp.float32) ** level_of(splits[5], (D, R), ((0, 256),), -0.2, 0.2)), 30.0, 3000.0)
    step_count = jax.random.randint(splits[6], (1,), 1, 11).astype(jnp.int32)
    return {"attn": attn, "cotangent": cotangent, "weight": weight, "projector": projector, "moment_one": moment_one, "moment_two": moment_two, "step_count": step_count}


def reference(attn, cotangent, weight, projector, moment_one, moment_two, step_count):
    reduced = jnp.dot(attn, projector, preferred_element_type=jnp.float32).astype(jnp.bfloat16)
    grad_input = lax.dot_general(cotangent, weight, (((1,), (1,)), ((), ())), preferred_element_type=jnp.float32).astype(jnp.bfloat16)
    projected = lax.dot_general(cotangent, reduced, (((0,), (0,)), ((), ())), preferred_element_type=jnp.float32)
    first_moment = 0.9 * moment_one + 0.1 * projected
    second_moment = 0.999 * moment_two + 0.001 * projected * projected
    steps = step_count[0].astype(jnp.float32)
    first_hat = first_moment / (1.0 - jnp.power(jnp.float32(0.9), steps))
    second_hat = second_moment / (1.0 - jnp.power(jnp.float32(0.999), steps))
    low_step = (first_hat / (jnp.sqrt(second_hat) + 1e-08)).astype(jnp.bfloat16)
    weight_step = 0.25 * lax.dot_general(projector, low_step, (((1,), (1,)), ((), ())), preferred_element_type=jnp.float32)
    return (grad_input, weight_step, first_moment, second_moment)
```

```python
import functools

import jax
import jax.numpy as jnp
from jax import lax
from jax.experimental import pallas as pl
from jax.experimental.pallas import tpu as pltpu
from jax.sharding import PartitionSpec as P

MESH = pl.DeviceIdType.MESH
F32 = jnp.float32
BF16 = jnp.bfloat16
NX = 4
NY = 4


def kernel(
    nz, unit,
    attn_hbm, cot_hbm, w_hbm, proj_hbm, m1_hbm, m2_hbm, step_ref,
    gi_hbm, ws_hbm, fm_hbm, sm_hbm,
    attn, cot, wfull, proj, reduced, pown, csend, crecv, xsend, xrecv, zsend, zrecv, yrecv,
    m1, m2, fm, sm, low, gi, ws,
    load_sem, cload_sem, out_sem,
    c_ss, c_rs, x_ss, x_rs, z_ss, z_rs, y_ss, y_rs, m_ss, m_rs,
    lz_ss, lz_rs, lx_ss, lx_rs, lc_ss, lc_rs,
    wy_ss, wy_rs, wy2_ss, wy2_rs, wx_ss, wx_rs, wc_ss, wc_rs,
):
    rows = 4 * unit
    zrows = 8 * rows
    dp, fs = lax.axis_index("dp"), lax.axis_index("fsdp")
    z, xh, c = dp // 4, (dp // 2) % 2, dp % 2
    xl, y = fs // NY, fs % NY
    x = xh * 2 + xl
    oc = 1 - c

    def device(z_, x_, c_, y_):
        return (z_ * 4 + (x_ // 2) * 2 + c_, (x_ % 2) * NY + y_)

    sibling = device(z, x, oc, y)
    xdev = [None] + [device(z, (x + k) % NX, c, y) for k in (1, 2, 3)]
    ydev = [None] + [device(z, x, c, (y + k) % NY) for k in (1, 2, 3)]
    zdev = [None] + [device((z + k) % nz, x, c, y) for k in range(1, nz)]

    def remote(src, dst, ss, rs, dev):
        return pltpu.make_async_remote_copy(
            src_ref=src, dst_ref=dst, send_sem=ss, recv_sem=rs, device_id=dev, device_id_type=MESH
        )

    sent = []

    def send(*args):
        copy = remote(*args)
        copy.start()
        sent.append(copy)

    load_proj = pltpu.make_async_copy(proj_hbm, proj, load_sem.at[0])
    load_attn = pltpu.make_async_copy(attn_hbm, attn, load_sem.at[1])
    load_proj.start()
    load_attn.start()

    def load_cot(i):
        cols = pl.ds(pl.multiple_of(i * zrows, 128), zrows)
        return pltpu.make_async_copy(cot_hbm.at[:, cols], cot.at[:, cols], cload_sem.at[i])

    for i in range(nz):
        load_cot(i).start()
    own = xl * NY + y
    load_w = pltpu.make_async_copy(w_hbm, wfull.at[own], load_sem.at[2])
    load_w.start()
    load_m1 = pltpu.make_async_copy(m1_hbm, m1.at[y], load_sem.at[3])
    load_m2 = pltpu.make_async_copy(m2_hbm, m2.at[y], load_sem.at[4])
    load_m1.start()
    load_m2.start()

    barrier = pltpu.get_barrier_semaphore()
    partners = [sibling] + xdev[1:] + ydev[1:] + zdev[1:]
    for dev in partners:
        pl.semaphore_signal(barrier, inc=1, device_id=dev, device_id_type=MESH)
    pl.semaphore_wait(barrier, len(partners))

    yp, ym, xp, xm = ydev[1], ydev[3], xdev[1], xdev[3]

    def shard(other, dy):
        return ((1 - xl) if other else xl) * NY + (y + dy) % NY

    send(w_hbm.at[c], wfull.at[own, c], wy_ss.at[0], wy_rs.at[0], yp)
    send(w_hbm.at[c], wfull.at[own, c], wy_ss.at[1], wy_rs.at[1], ym)

    def weight_x(dy, src0, src1):
        s = shard(False, dy)
        send(src0, wfull.at[s, c, 0], wx_ss.at[dy, 0], wx_rs.at[dy, 0], xp)
        send(src1, wfull.at[s, c, 1], wx_ss.at[dy, 1], wx_rs.at[dy, 1], xm)

    def weight_core(other, dy):
        s = shard(other, dy)
        part = wfull.at[s, c]
        send(part, part, wc_ss.at[other, dy], wc_rs.at[other, dy], sibling)

    def weight_core_wait(other, dy):
        part = wfull.at[shard(other, dy), oc]
        remote(part, part, wc_ss.at[other, dy], wc_rs.at[other, dy], sibling).wait_recv()

    weight_x(0, w_hbm.at[c, 0], w_hbm.at[c, 1])

    for k in (1, 2, 3):
        send(m1_hbm, m1.at[y], m_ss.at[0, k - 1], m_rs.at[0, k - 1], ydev[k])
        send(m2_hbm, m2.at[y], m_ss.at[1, k - 1], m_rs.at[1, k - 1], ydev[k])

    load_proj.wait()
    load_attn.wait()
    reduced[...] = jnp.dot(attn[...], proj[...], preferred_element_type=F32).astype(BF16)

    def core_copy(i):
        return remote(csend.at[i], crecv.at[i], c_ss.at[i], c_rs.at[i], sibling)

    def part_step(i, carry):
        load_cot(i).wait()
        cols = pl.ds(pl.multiple_of(i * zrows, 128), zrows)
        part = lax.dot_general(
            cot[:, cols], reduced[...], (((0,), (0,)), ((), ())), preferred_element_type=F32
        ).reshape(2, 2, 2 * rows, -1)
        mine = c == 0
        pown[i] = jnp.where(mine, part[:, 0], part[:, 1])
        csend[i] = jnp.where(mine, part[:, 1], part[:, 0]).astype(BF16)
        core_copy(i).start()
        return carry

    lax.fori_loop(0, nz, part_step, 0)

    half = nz // 2

    def x_sum(i, carry):
        core_copy(i).wait_recv()
        total = (pown[i] + crecv[i].astype(F32)).astype(BF16).reshape(4, rows, -1)
        for k in range(4):
            xsend[k, i] = total[k]
        return carry

    for h in range(2):
        lax.fori_loop(h * half, (h + 1) * half, x_sum, 0)
        part = pl.ds(h * half, half)
        for k in (1, 3, 2):
            send(
                xsend.at[(x + k) % NX, part], xrecv.at[x, part],
                x_ss.at[h, k - 1], x_rs.at[h, k - 1], xdev[k],
            )

    def from_y(k):
        s = wfull.at[shard(False, k), c]
        remote(s, s, wy_ss.at[0], wy_rs.at[0 if k == 3 else 1], ydev[k]).wait_recv()

    from_y(3)
    part = wfull.at[shard(False, 3), c, 0]
    send(part, part, wy2_ss.at[0], wy2_rs.at[0], yp)
    from_y(1)
    part = wfull.at[shard(False, 1), c, 1]
    send(part, part, wy2_ss.at[1], wy2_rs.at[1], ym)
    for dy in (3, 1):
        s = shard(False, dy)
        weight_x(dy, wfull.at[s, c, 0], wfull.at[s, c, 1])
        weight_core(0, dy)

    for h in range(2):
        part = pl.ds(h * half, half)
        for k in (1, 2, 3):
            slot = xrecv.at[(x + k) % NX, part]
            remote(slot, slot, x_ss.at[h, 0], x_rs.at[h, 3 - k], xdev[k]).wait_recv()

    def z_sum(i, carry):
        total = xsend[x, i].astype(F32)
        for k in (1, 2, 3):
            total += xrecv[(x + k) % NX, i].astype(F32)
        zsend[i] = total.astype(BF16)
        return carry

    lax.fori_loop(0, nz, z_sum, 0)
    for k in range(1, nz):
        send(zsend.at[(z + k) % nz], zrecv.at[z], z_ss.at[k - 1], z_rs.at[k - 1], zdev[k])

    s2 = shard(False, 2)
    part = wfull.at[s2, c, 0]
    remote(part, part, wy2_ss.at[0], wy2_rs.at[0], ym).wait_recv()
    part = wfull.at[s2, c, 1]
    remote(part, part, wy2_ss.at[1], wy2_rs.at[1], yp).wait_recv()
    weight_x(2, wfull.at[s2, c, 0], wfull.at[s2, c, 1])
    weight_core(0, 2)

    for k in range(1, nz):
        slot = zrecv.at[(z + k) % nz]
        remote(slot, slot, z_ss.at[0], z_rs.at[nz - 1 - k], zdev[k]).wait_recv()
    total = zsend[z].astype(F32)
    for k in range(1, nz):
        total += zrecv[(z + k) % nz].astype(F32)
    yrecv[y] = total.astype(BF16)
    for k in (1, 2, 3):
        send(yrecv.at[y], yrecv.at[y], y_ss.at[k - 1], y_rs.at[k - 1], ydev[k])

    load_w.wait()
    load_m1.wait()
    load_m2.wait()

    grad_copies = []

    def grad(other, pair):
        q = ((1 - xl) if other else xl) * 2 + pair
        w = wfull[pl.ds(2 * q, 2)].reshape(-1, wfull.shape[-1])
        width = w.shape[0]
        gi[q] = lax.dot_general(
            cot[...], w, (((1,), (1,)), ((), ())), preferred_element_type=F32
        ).astype(BF16)
        cols = pl.ds(pl.multiple_of(q * width, 128), width)
        copy = pltpu.make_async_copy(gi.at[q], gi_hbm.at[:, cols], out_sem.at[2 * other + pair])
        copy.start()
        grad_copies.append(copy)

    for dy in (1, 2, 3):
        weight_core_wait(0, dy)
    grad(0, 0)

    for k in (1, 2, 3):
        slot = yrecv.at[(y + k) % NY]
        remote(slot, slot, y_ss.at[0], y_rs.at[3 - k], ydev[k]).wait_recv()
        for j, m in enumerate((m1, m2)):
            slot = m.at[(y + k) % NY]
            remote(slot, slot, m_ss.at[j, 0], m_rs.at[j, 3 - k], ydev[k]).wait_recv()
    projected = (
        yrecv[0].astype(F32) + yrecv[1].astype(F32) + yrecv[2].astype(F32) + yrecv[3].astype(F32)
    )
    projected = projected.reshape(NY, unit, -1)
    first = 0.9 * m1[...] + 0.1 * projected
    second = 0.999 * m2[...] + 0.001 * projected * projected
    fm[...] = first
    sm[...] = second
    steps = jnp.full((1, first.shape[-1]), step_ref[0], jnp.int32).astype(F32)
    first_hat = first / (1.0 - jnp.power(F32(0.9), steps))
    second_hat = second / (1.0 - jnp.power(F32(0.999), steps))
    low_step = first_hat / (jnp.sqrt(second_hat) + 1e-08)
    low[z, xh, c, xl] = low_step.reshape(rows, -1).astype(BF16)
    mine = low.at[z, xh, c, xl]
    for k in range(1, nz):
        send(mine, mine, lz_ss.at[k - 1], lz_rs.at[k - 1], zdev[k])
    store_fm = pltpu.make_async_copy(fm.at[y], fm_hbm, load_sem.at[3])
    store_sm = pltpu.make_async_copy(sm.at[y], sm_hbm, load_sem.at[4])
    store_fm.start()
    store_sm.start()

    for dy in (0, 3, 1, 2):
        s = shard(True, dy)
        for q, dev in ((0, xm), (1, xp)):
            part = wfull.at[s, c, q]
            remote(part, part, wx_ss.at[dy, q], wx_rs.at[dy, q], dev).wait_recv()
        weight_core(1, dy)

    for k in range(1, nz):
        slot = low.at[(z + k) % nz, xh, c, xl]
        remote(slot, slot, lz_ss.at[0], lz_rs.at[nz - 1 - k], zdev[k]).wait_recv()
    mine = low.at[:, xh, c, xl]
    for k in (1, 3, 2):
        send(mine, mine, lx_ss.at[k - 1], lx_rs.at[k - 1], xdev[k])
    send(mine, mine, lc_ss.at[0], lc_rs.at[0], sibling)

    grad(0, 1)

    for k in (1, 2, 3):
        x_ = (x + k) % NX
        slot = low.at[:, x_ // 2, c, x_ % 2]
        remote(slot, slot, lx_ss.at[0], lx_rs.at[3 - k], xdev[k]).wait_recv()
        send(slot, slot, lc_ss.at[k], lc_rs.at[k], sibling)

    for dy in range(4):
        weight_core_wait(1, dy)
    grad(1, 0)

    for k in range(4):
        x_ = (x + k) % NX
        slot = low.at[:, x_ // 2, oc, x_ % 2]
        remote(slot, slot, lc_ss.at[k], lc_rs.at[k], sibling).wait_recv()

    span = ws.shape[0]
    mine_proj = proj[pl.ds(pl.multiple_of(fs * span, 64), span), :]

    def ws_copy(i):
        cols = pl.ds(pl.multiple_of(i * zrows, 128), zrows)
        return pltpu.make_async_copy(ws.at[:, cols], ws_hbm.at[:, cols], cload_sem.at[i])

    def ws_step(i, carry):
        cols = pl.ds(pl.multiple_of(i * zrows, 128), zrows)
        ws[:, cols] = 0.25 * lax.dot_general(
            mine_proj, low[i].reshape(zrows, -1), (((1,), (1,)), ((), ())),
            preferred_element_type=F32,
        )
        ws_copy(i).start()
        return carry

    lax.fori_loop(0, nz, ws_step, 0)
    grad(1, 1)

    for copy in sent:
        copy.wait_send()

    def finish(i, carry):
        core_copy(i).wait_send()
        ws_copy(i).wait()
        return carry

    lax.fori_loop(0, nz, finish, 0)
    for copy in grad_copies:
        copy.wait()
    store_fm.wait()
    store_sm.wait()


def on_device(nz, attn, cot, w, proj, m1, m2, steps):
    unit, rank = m1.shape
    tokens, inner = attn.shape
    width = cot.shape[1]
    rows = 4 * unit
    span = w.shape[0]
    q = span // 4
    dma = pltpu.SemaphoreType.DMA
    vm = pltpu.VMEM
    any_ = pl.BlockSpec(memory_space=pl.ANY)
    gi, ws, fm, sm = pl.pallas_call(
        functools.partial(kernel, nz, unit),
        out_shape=(
            jax.ShapeDtypeStruct((tokens, inner), BF16),
            jax.ShapeDtypeStruct((span, width), F32),
            jax.ShapeDtypeStruct(m1.shape, F32),
            jax.ShapeDtypeStruct(m2.shape, F32),
        ),
        in_specs=[any_] * 6 + [pl.BlockSpec(memory_space=pltpu.SMEM)],
        out_specs=(any_,) * 4,
        scratch_shapes=[
            vm((tokens, inner), BF16),
            vm((tokens, width), BF16),
            vm((8, 2, 2, q, width), BF16),
            vm((inner, rank), BF16),
            vm((tokens, rank), BF16),
            vm((nz, 2, 2 * rows, rank), F32),
            vm((nz, 2, 2 * rows, rank), BF16),
            vm((nz, 2, 2 * rows, rank), BF16),
            vm((4, nz, rows, rank), BF16),
            vm((4, nz, rows, rank), BF16),
            vm((nz, rows, rank), BF16),
            vm((nz, rows, rank), BF16),
            vm((4, rows, rank), BF16),
            vm((4, unit, rank), F32),
            vm((4, unit, rank), F32),
            vm((4, unit, rank), F32),
            vm((4, unit, rank), F32),
            vm((nz, 2, 2, 2, rows, rank), BF16),
            vm((4, tokens, 2 * span), BF16),
            vm((span, width), F32),
            dma((5,)), dma((nz,)), dma((4,)),
            dma((nz,)), dma((nz,)),
            dma((2, 3)), dma((2, 3)),
            dma((nz - 1,)), dma((nz - 1,)),
            dma((3,)), dma((3,)),
            dma((2, 3)), dma((2, 3)),
            dma((nz - 1,)), dma((nz - 1,)),
            dma((3,)), dma((3,)),
            dma((4,)), dma((4,)),
            dma((2,)), dma((2,)),
            dma((2,)), dma((2,)),
            dma((4, 2)), dma((4, 2)),
            dma((2, 4)), dma((2, 4)),
        ],
        compiler_params=pltpu.CompilerParams(
            collective_id=0, has_side_effects=True, vmem_limit_bytes=56 * 2**20
        ),
    )(attn, cot, w.reshape(2, 2, q, width), proj, m1, m2, steps)
    return gi, ws, fm, sm


def solution(mesh):
    placed = (
        P(("dp", "fsdp"), None),
        P(("dp", "fsdp"), None),
        P("fsdp", None),
        P(),
        P(("dp", "fsdp"), None),
        P(("dp", "fsdp"), None),
        P(),
    )
    return jax.shard_map(
        functools.partial(on_device, mesh.shape["dp"] // 4),
        mesh=mesh,
        in_specs=placed,
        out_specs=(
            P(("dp", "fsdp"), None),
            P("fsdp", None),
            P(("dp", "fsdp"), None),
            P(("dp", "fsdp"), None),
        ),
        check_vma=False,
    )
```

```python
import functools

import jax
import jax.numpy as jnp
from jax import lax
from jax.experimental import pallas as pl
from jax.experimental.pallas import tpu as pltpu
from jax.sharding import PartitionSpec as P

MESH = pl.DeviceIdType.MESH
F32 = jnp.float32
BF16 = jnp.bfloat16
NX = 4
NY = 4


def kernel(
    nz, unit,
    attn_hbm, cot_hbm, w_hbm, proj_hbm, m1_hbm, m2_hbm, step_ref,
    gi, low, proj_mine, fm_mine, sm_mine,
    attn, cot, wfull, proj, reduced, pown, csend, crecv, xsend, xrecv, zsend, zrecv, yrecv,
    m1, m2, fm, sm,
    load_sem, cload_sem,
    c_ss, c_rs, x_ss, x_rs, z_ss, z_rs, y_ss, y_rs, m_ss, m_rs,
    lz_ss, lz_rs, lx_ss, lx_rs, ly_ss, ly_rs, lc_ss, lc_rs,
    wy_ss, wy_rs, wy2_ss, wy2_rs, wx_ss, wx_rs, wz_ss, wz_rs, wc_ss, wc_rs, wo_ss, wo_rs,
):
    rows = 4 * unit
    zrows = 8 * rows
    dp, fs = lax.axis_index("dp"), lax.axis_index("fsdp")
    z, xh, c = dp // 4, (dp // 2) % 2, dp % 2
    xl, y = fs // NY, fs % NY
    x = xh * 2 + xl
    oc = 1 - c

    def device(z_, x_, c_, y_):
        return (z_ * 4 + (x_ // 2) * 2 + c_, (x_ % 2) * NY + y_)

    sibling = device(z, x, oc, y)
    xdev = [None] + [device(z, (x + k) % NX, c, y) for k in (1, 2, 3)]
    ydev = [None] + [device(z, x, c, (y + k) % NY) for k in (1, 2, 3)]
    zdev = [None] + [device((z + k) % nz, x, c, y) for k in range(1, nz)]

    def remote(src, dst, ss, rs, dev):
        return pltpu.make_async_remote_copy(
            src_ref=src, dst_ref=dst, send_sem=ss, recv_sem=rs, device_id=dev, device_id_type=MESH
        )

    sent = []

    def send(*args):
        copy = remote(*args)
        copy.start()
        sent.append(copy)

    load_proj = pltpu.make_async_copy(proj_hbm, proj, load_sem.at[0])
    load_attn = pltpu.make_async_copy(attn_hbm, attn, load_sem.at[1])
    load_proj.start()
    load_attn.start()

    def load_cot(i):
        cols = pl.ds(pl.multiple_of(i * zrows, 128), zrows)
        return pltpu.make_async_copy(cot_hbm.at[:, cols], cot.at[:, cols], cload_sem.at[i])

    for i in range(nz):
        load_cot(i).start()
    own = xl * NY + y
    load_w = pltpu.make_async_copy(w_hbm, wfull.at[own], load_sem.at[2])
    load_w.start()
    load_m1 = pltpu.make_async_copy(m1_hbm, m1.at[y], load_sem.at[3])
    load_m2 = pltpu.make_async_copy(m2_hbm, m2.at[y], load_sem.at[4])
    load_m1.start()
    load_m2.start()

    barrier = pltpu.get_barrier_semaphore()
    partners = [sibling] + xdev[1:] + ydev[1:] + zdev[1:]
    for dev in partners:
        pl.semaphore_signal(barrier, inc=1, device_id=dev, device_id_type=MESH)
    pl.semaphore_wait(barrier, len(partners))

    yp, ym, xp, xm, zp, zm = ydev[1], ydev[3], xdev[1], xdev[3], zdev[1], zdev[nz - 1]
    rx = z % 2
    rz = 1 - rx
    hcol = w_hbm.shape[-1] // 2
    colh = [pl.ds(0, hcol), pl.ds(hcol, hcol)]

    def shard(other, dy):
        return ((1 - xl) if other else xl) * NY + (y + dy) % NY

    def weight_x(dy, from_hbm=False):
        s = shard(False, dy)
        for j, dev in ((0, xp), (1, xm)):
            src = w_hbm.at[c, rx, :, colh[j]] if from_hbm else wfull.at[s, c, rx, :, colh[j]]
            send(src, wfull.at[s, c, rx, :, colh[j]], wx_ss.at[dy, j], wx_rs.at[dy, j], dev)

    def weight_x_to_z(dy):
        s = shard(True, dy)
        for j, src, dst in ((0, xm, zp), (1, xp, zm)):
            part = wfull.at[s, c, rx, :, colh[j]]
            remote(part, part, wx_ss.at[dy, j], wx_rs.at[dy, j], src).wait_recv()
            send(part, part, wz_ss.at[dy, j], wz_rs.at[dy, j], dst)
        part = wfull.at[s, c, rx]
        send(part, part, wo_ss.at[dy, 0], wo_rs.at[dy, 0], sibling)

    def weight_z_to_core(dy):
        s = shard(True, dy)
        for j, src in ((0, zm), (1, zp)):
            part = wfull.at[s, c, rz, :, colh[j]]
            remote(part, part, wz_ss.at[dy, j], wz_rs.at[dy, j], src).wait_recv()
        part = wfull.at[s, c, rz]
        send(part, part, wo_ss.at[dy, 1], wo_rs.at[dy, 1], sibling)

    def weight_core(dy):
        part = wfull.at[shard(False, dy), c]
        send(part, part, wc_ss.at[dy - 1], wc_rs.at[dy - 1], sibling)

    def weight_core_wait(other, dy):
        s = shard(other, dy)
        if other:
            for i, r in enumerate((rx, rz)):
                part = wfull.at[s, oc, r]
                remote(part, part, wo_ss.at[dy, i], wo_rs.at[dy, i], sibling).wait_recv()
        else:
            part = wfull.at[s, oc]
            remote(part, part, wc_ss.at[dy - 1], wc_rs.at[dy - 1], sibling).wait_recv()

    for i in range(2):
        for d, dev in ((0, yp), (1, ym)):
            r = i if d == 0 else 1 - i
            send(w_hbm.at[c, r], wfull.at[own, c, r], wy_ss.at[d, r], wy_rs.at[d, r], dev)
    weight_x(0, True)

    for k in (1, 2, 3):
        send(m1_hbm, m1.at[y], m_ss.at[0, k - 1], m_rs.at[0, k - 1], ydev[k])
        send(m2_hbm, m2.at[y], m_ss.at[1, k - 1], m_rs.at[1, k - 1], ydev[k])

    load_proj.wait()
    load_attn.wait()
    reduced[...] = jnp.dot(attn[...], proj[...], preferred_element_type=F32).astype(BF16)

    def core_copy(i):
        return remote(csend.at[i], crecv.at[i], c_ss.at[i], c_rs.at[i], sibling)

    def part_step(i, carry):
        load_cot(i).wait()
        cols = pl.ds(pl.multiple_of(i * zrows, 128), zrows)
        part = lax.dot_general(
            cot[:, cols], reduced[...], (((0,), (0,)), ((), ())), preferred_element_type=F32
        ).reshape(2, 2, 2 * rows, -1)
        mine = c == 0
        pown[i] = jnp.where(mine, part[:, 0], part[:, 1])
        csend[i] = jnp.where(mine, part[:, 1], part[:, 0]).astype(BF16)
        core_copy(i).start()
        return carry

    lax.fori_loop(0, nz, part_step, 0)

    half = nz // 2

    def x_sum(i, carry):
        core_copy(i).wait_recv()
        total = (pown[i] + crecv[i].astype(F32)).astype(BF16).reshape(4, rows, -1)
        for k in range(4):
            xsend[k, i] = total[k]
        return carry

    for h in range(2):
        lax.fori_loop(h * half, (h + 1) * half, x_sum, 0)
        part = pl.ds(h * half, half)
        for k in (1, 3, 2):
            send(
                xsend.at[(x + k) % NX, part], xrecv.at[x, part],
                x_ss.at[h, k - 1], x_rs.at[h, k - 1], xdev[k],
            )

    def from_y(k, r):
        part = wfull.at[shard(False, k), c, r]
        d = 0 if k == 3 else 1
        remote(part, part, wy_ss.at[d, r], wy_rs.at[d, r], ydev[k]).wait_recv()
        return part

    part = from_y(3, 0)
    send(part, part, wy2_ss.at[0], wy2_rs.at[0], yp)
    part = from_y(1, 1)
    send(part, part, wy2_ss.at[1], wy2_rs.at[1], ym)
    weight_x_to_z(0)
    from_y(3, 1)
    weight_x(3)
    weight_core(3)
    from_y(1, 0)
    weight_x(1)
    weight_core(1)

    for h in range(2):
        part = pl.ds(h * half, half)
        for k in (1, 2, 3):
            slot = xrecv.at[(x + k) % NX, part]
            remote(slot, slot, x_ss.at[h, 0], x_rs.at[h, 3 - k], xdev[k]).wait_recv()

    def z_sum(i, carry):
        total = xsend[x, i].astype(F32)
        for k in (1, 2, 3):
            total += xrecv[(x + k) % NX, i].astype(F32)
        zsend[i] = total.astype(BF16)
        return carry

    lax.fori_loop(0, nz, z_sum, 0)
    for k in range(1, nz):
        send(zsend.at[(z + k) % nz], zrecv.at[z], z_ss.at[k - 1], z_rs.at[k - 1], zdev[k])

    s2 = shard(False, 2)
    for r, dev in ((0, ym), (1, yp)):
        part = wfull.at[s2, c, r]
        remote(part, part, wy2_ss.at[r], wy2_rs.at[r], dev).wait_recv()
    weight_x(2)
    weight_core(2)
    weight_x_to_z(3)
    weight_x_to_z(1)

    for k in range(1, nz):
        slot = zrecv.at[(z + k) % nz]
        remote(slot, slot, z_ss.at[0], z_rs.at[nz - 1 - k], zdev[k]).wait_recv()
    total = zsend[z].astype(F32)
    for k in range(1, nz):
        total += zrecv[(z + k) % nz].astype(F32)
    yrecv[y] = total.astype(BF16)
    for k in (1, 2, 3):
        send(yrecv.at[y], yrecv.at[y], y_ss.at[k - 1], y_rs.at[k - 1], ydev[k])

    load_w.wait()
    load_m1.wait()
    load_m2.wait()

    def grad(other, pair):
        q = ((1 - xl) if other else xl) * 2 + pair
        w = wfull[pl.ds(2 * q, 2)].reshape(-1, wfull.shape[-1])
        gi[q] = lax.dot_general(
            cot[...], w, (((1,), (1,)), ((), ())), preferred_element_type=F32
        ).astype(BF16)

    for dy in (1, 2, 3):
        weight_core_wait(0, dy)
    grad(0, 0)

    for k in (1, 2, 3):
        slot = yrecv.at[(y + k) % NY]
        remote(slot, slot, y_ss.at[0], y_rs.at[3 - k], ydev[k]).wait_recv()
        for j, m in enumerate((m1, m2)):
            slot = m.at[(y + k) % NY]
            remote(slot, slot, m_ss.at[j, 0], m_rs.at[j, 3 - k], ydev[k]).wait_recv()
    projected = (
        yrecv[0].astype(F32) + yrecv[1].astype(F32) + yrecv[2].astype(F32) + yrecv[3].astype(F32)
    )
    projected = projected.reshape(NY, unit, -1)
    first = 0.9 * m1[...] + 0.1 * projected
    second = 0.999 * m2[...] + 0.001 * projected * projected
    fm[...] = first
    sm[...] = second
    steps = jnp.full((1, first.shape[-1]), step_ref[0], jnp.int32).astype(F32)
    first_hat = first / (1.0 - jnp.power(F32(0.9), steps))
    second_hat = second / (1.0 - jnp.power(F32(0.999), steps))
    low_step = first_hat / (jnp.sqrt(second_hat) + 1e-08)
    low_step = low_step.reshape(rows, -1).astype(BF16)
    rank_half = low_step.shape[-1] // 2
    jy = y % 2
    low[jy, z, xh, c, xl] = jnp.where(jy == 0, low_step[:, :rank_half], low_step[:, rank_half:])
    mine = low.at[jy, z, xh, c, xl]
    for k in range(1, nz):
        send(mine, mine, lz_ss.at[k - 1], lz_rs.at[k - 1], zdev[k])
    fm_mine[...] = fm[y]
    sm_mine[...] = sm[y]
    span = proj_mine.shape[0]
    proj_mine[...] = proj[pl.ds(pl.multiple_of(fs * span, 64), span), :]

    weight_x_to_z(2)
    for dy in (0, 3, 1):
        weight_z_to_core(dy)

    for k in range(1, nz):
        slot = low.at[jy, (z + k) % nz, xh, c, xl]
        remote(slot, slot, lz_ss.at[0], lz_rs.at[nz - 1 - k], zdev[k]).wait_recv()

    def low_part(j, k, c_):
        x_ = (x + k) % NX
        return low.at[j, :, x_ // 2, c_, x_ % 2]

    def low_zhalf(j, k, h):
        x_ = (x + k) % NX
        return low.at[j, pl.ds(h * half, half), x_ // 2, c, x_ % 2]

    def low_spread(k):
        for h, dev in ((0, yp), (1, ym)):
            part = low_zhalf(jy, k, h)
            send(part, part, ly_ss.at[k, h], ly_rs.at[k, h], dev)
        part = low_part(jy, k, c)
        send(part, part, lc_ss.at[0, k], lc_rs.at[0, k], sibling)

    mine = low_part(jy, 0, c)
    for k in (1, 3, 2):
        send(mine, mine, lx_ss.at[k - 1], lx_rs.at[k - 1], xdev[k])
    low_spread(0)

    grad(0, 1)
    weight_z_to_core(2)

    for k in (1, 3, 2):
        slot = low_part(jy, k, c)
        remote(slot, slot, lx_ss.at[0], lx_rs.at[3 - k], xdev[k]).wait_recv()
        low_spread(k)

    for dy in range(4):
        weight_core_wait(1, dy)
    grad(1, 0)

    for k in (0, 1, 3, 2):
        for h, dev in ((0, ym), (1, yp)):
            part = low_zhalf(1 - jy, k, h)
            remote(part, part, ly_ss.at[k, h], ly_rs.at[k, h], dev).wait_recv()
        part = low_part(1 - jy, k, c)
        send(part, part, lc_ss.at[1, k], lc_rs.at[1, k], sibling)

    grad(1, 1)

    for k in range(4):
        for i, j in ((0, jy), (1, 1 - jy)):
            slot = low_part(j, k, oc)
            remote(slot, slot, lc_ss.at[i, k], lc_rs.at[i, k], sibling).wait_recv()

    for copy in sent:
        copy.wait_send()

    def finish(i, carry):
        core_copy(i).wait_send()
        return carry

    lax.fori_loop(0, nz, finish, 0)


def finish_kernel(gi, low, proj, fm, sm, gi_hbm, ws_hbm, fm_hbm, sm_hbm, ws, gi_sem, ws_sem, m_sem):
    nz = low.shape[1]
    width = gi.shape[-1]
    copies = [
        pltpu.make_async_copy(gi.at[q], gi_hbm.at[:, pl.ds(q * width, width)], gi_sem.at[q])
        for q in range(4)
    ]
    copies.append(pltpu.make_async_copy(fm, fm_hbm, m_sem.at[0]))
    copies.append(pltpu.make_async_copy(sm, sm_hbm, m_sem.at[1]))
    for copy in copies:
        copy.start()
    zrows = ws.shape[1] // nz

    def ws_copy(i):
        cols = pl.ds(pl.multiple_of(i * zrows, 128), zrows)
        return pltpu.make_async_copy(ws.at[:, cols], ws_hbm.at[:, cols], ws_sem.at[i])

    def ws_step(i, carry):
        cols = pl.ds(pl.multiple_of(i * zrows, 128), zrows)
        rows = jnp.concatenate([low[j, i].reshape(zrows, -1) for j in range(2)], axis=1)
        ws[:, cols] = 0.25 * lax.dot_general(
            proj[...], rows, (((1,), (1,)), ((), ())), preferred_element_type=F32
        )
        ws_copy(i).start()
        return carry

    lax.fori_loop(0, nz, ws_step, 0)

    def ws_wait(i, carry):
        ws_copy(i).wait()
        return carry

    lax.fori_loop(0, nz, ws_wait, 0)
    for copy in copies:
        copy.wait()


def on_device(nz, attn, cot, w, proj, m1, m2, steps):
    unit, rank = m1.shape
    tokens, inner = attn.shape
    width = cot.shape[1]
    rows = 4 * unit
    span = w.shape[0]
    q = span // 4
    dma = pltpu.SemaphoreType.DMA
    vm = pltpu.VMEM
    any_ = pl.BlockSpec(memory_space=pl.ANY)
    results = pl.pallas_call(
        functools.partial(kernel, nz, unit),
        out_shape=(
            vm((4, tokens, 2 * span), BF16),
            vm((2, nz, 2, 2, 2, rows, rank // 2), BF16),
            vm((span, rank), BF16),
            vm(m1.shape, F32),
            vm(m2.shape, F32),
        ),
        in_specs=[pl.BlockSpec(memory_space=pltpu.HBM)] * 6 + [pl.BlockSpec(memory_space=pltpu.SMEM)],
        out_specs=(pl.BlockSpec(memory_space=vm),) * 5,
        scratch_shapes=[
            vm((tokens, inner), BF16),
            vm((tokens, width), BF16),
            vm((8, 2, 2, q, width), BF16),
            vm((inner, rank), BF16),
            vm((tokens, rank), BF16),
            vm((nz, 2, 2 * rows, rank), F32),
            vm((nz, 2, 2 * rows, rank), BF16),
            vm((nz, 2, 2 * rows, rank), BF16),
            vm((4, nz, rows, rank), BF16),
            vm((4, nz, rows, rank), BF16),
            vm((nz, rows, rank), BF16),
            vm((nz, rows, rank), BF16),
            vm((4, rows, rank), BF16),
            vm((4, unit, rank), F32),
            vm((4, unit, rank), F32),
            vm((4, unit, rank), F32),
            vm((4, unit, rank), F32),
            dma((5,)), dma((nz,)),
            dma((nz,)), dma((nz,)),
            dma((2, 3)), dma((2, 3)),
            dma((nz - 1,)), dma((nz - 1,)),
            dma((3,)), dma((3,)),
            dma((2, 3)), dma((2, 3)),
            dma((nz - 1,)), dma((nz - 1,)),
            dma((3,)), dma((3,)),
            dma((4, 2)), dma((4, 2)),
            dma((2, 4)), dma((2, 4)),
            dma((2, 2)), dma((2, 2)),
            dma((2,)), dma((2,)),
            dma((4, 2)), dma((4, 2)),
            dma((4, 2)), dma((4, 2)),
            dma((3,)), dma((3,)),
            dma((4, 2)), dma((4, 2)),
        ],
        compiler_params=pltpu.CompilerParams(
            collective_id=0, has_side_effects=True, vmem_limit_bytes=40 * 2**20
        ),
    )(
        *(
            pltpu.with_memory_space_constraint(a, pltpu.HBM)
            for a in (attn, cot, w.reshape(2, 2, q, width), proj, m1, m2)
        ),
        steps,
    )
    return pl.pallas_call(
        finish_kernel,
        out_shape=(
            jax.ShapeDtypeStruct((tokens, inner), BF16),
            jax.ShapeDtypeStruct((span, width), F32),
            jax.ShapeDtypeStruct(m1.shape, F32),
            jax.ShapeDtypeStruct(m2.shape, F32),
        ),
        in_specs=[pl.BlockSpec(memory_space=vm)] * 5,
        out_specs=(any_,) * 4,
        scratch_shapes=[vm((span, width), F32), dma((4,)), dma((nz,)), dma((2,))],
        compiler_params=pltpu.CompilerParams(vmem_limit_bytes=16 * 2**20),
    )(*(pltpu.with_memory_space_constraint(a, vm) for a in results))


def solution(mesh):
    placed = (
        P(("dp", "fsdp"), None),
        P(("dp", "fsdp"), None),
        P("fsdp", None),
        P(),
        P(("dp", "fsdp"), None),
        P(("dp", "fsdp"), None),
        P(),
    )
    return jax.shard_map(
        functools.partial(on_device, mesh.shape["dp"] // 4),
        mesh=mesh,
        in_specs=placed,
        out_specs=(
            P(("dp", "fsdp"), None),
            P("fsdp", None),
            P(("dp", "fsdp"), None),
            P(("dp", "fsdp"), None),
        ),
        check_vma=False,
    )
```

```python
import functools

import jax
import jax.numpy as jnp
from jax import lax
from jax.experimental import pallas as pl
from jax.experimental.pallas import tpu as pltpu
from jax.sharding import PartitionSpec as P

MESH = pl.DeviceIdType.MESH
F32 = jnp.float32
BF16 = jnp.bfloat16
NX = 4
NY = 4


def kernel(
    nz, unit,
    attn_hbm, cot_hbm, w_hbm, proj_hbm, m1_hbm, m2_hbm, step_ref,
    gi, low, proj_mine, fm_mine, sm_mine,
    attn, cot, wfull, proj, reduced, pown, csend, crecv, fsend, frecv, gsend, grecv, zsend, zrecv,
    m1, m2, fm, sm,
    load_sem, cload_sem,
    c_ss, c_rs, f_ss, f_rs, g_ss, g_rs, z_ss, z_rs, m_ss, m_rs, o_ss, o_rs,
    lz_ss, lz_rs, lg_ss, lg_rs, lf_ss, lf_rs, lc_ss, lc_rs,
    wy_ss, wy_rs, wy2_ss, wy2_rs, wx_ss, wx_rs, wz_ss, wz_rs, wc_ss, wc_rs,
):
    rows = 4 * unit
    zrows = 8 * rows
    ne = nz // NY
    dp, fs = lax.axis_index("dp"), lax.axis_index("fsdp")
    z, xh, c = dp // 4, (dp // 2) % 2, dp % 2
    xl, y = fs // NY, fs % NY
    x = xh * 2 + xl
    oc = 1 - c
    fme = x * oc + y * c
    gme = y * oc + x * c
    owner = z // ne
    owns = y == owner

    def device(z_, x_, c_, y_):
        return (z_ * 4 + (x_ // 2) * 2 + c_, (x_ % 2) * NY + y_)

    sibling = device(z, x, oc, y)
    xdev = [None] + [device(z, (x + k) % NX, c, y) for k in (1, 2, 3)]
    ydev = [None] + [device(z, x, c, (y + k) % NY) for k in (1, 2, 3)]
    zdev = [None] + [device((z + k) % nz, x, c, y) for k in range(1, nz)]
    fdev = [None] + [device(z, (x + k * oc) % NX, c, (y + k * c) % NY) for k in (1, 2, 3)]
    gdev = [None] + [device(z, (x + k * c) % NX, c, (y + k * oc) % NY) for k in (1, 2, 3)]
    owner_dev = device(z, x, c, owner)

    def remote(src, dst, ss, rs, dev):
        return pltpu.make_async_remote_copy(
            src_ref=src, dst_ref=dst, send_sem=ss, recv_sem=rs, device_id=dev, device_id_type=MESH
        )

    def send(*args):
        remote(*args).start()

    def arrive(part, rs):
        remote(part, part, rs, rs, sibling).wait_recv()

    def left(part, ss):
        remote(part, part, ss, ss, sibling).wait_send()

    load_proj = pltpu.make_async_copy(proj_hbm, proj, load_sem.at[0])
    load_attn = pltpu.make_async_copy(attn_hbm, attn, load_sem.at[1])
    load_proj.start()
    load_attn.start()

    def load_cot(i):
        cols = pl.ds(pl.multiple_of(i * zrows, 128), zrows)
        return pltpu.make_async_copy(cot_hbm.at[:, cols], cot.at[:, cols], cload_sem.at[i])

    load_cot(0).start()
    load_cot(1).start()
    own = xl * NY + y
    load_w = pltpu.make_async_copy(w_hbm, wfull.at[own], load_sem.at[2])
    load_m1 = pltpu.make_async_copy(m1_hbm, m1.at[y], load_sem.at[3])
    load_m2 = pltpu.make_async_copy(m2_hbm, m2.at[y], load_sem.at[4])

    barrier = pltpu.get_barrier_semaphore()
    partners = [sibling] + xdev[1:] + ydev[1:] + zdev[1:]
    for dev in partners:
        pl.semaphore_signal(barrier, inc=1, device_id=dev, device_id_type=MESH)
    pl.semaphore_wait(barrier, len(partners))

    yp, ym, xp, xm, zp, zm = ydev[1], ydev[3], xdev[1], xdev[3], zdev[1], zdev[nz - 1]
    rx = z % 2
    rz = 1 - rx
    hcol = w_hbm.shape[-1] // 2
    colh = [pl.ds(0, hcol), pl.ds(hcol, hcol)]

    def shard(other, dy):
        return ((1 - xl) if other else xl) * NY + (y + dy) % NY

    def half_rows(other, dy, r):
        return wfull.at[shard(other, dy), c, r]

    def piece(other, dy, r, j):
        return wfull.at[shard(other, dy), c, r, :, colh[j]]

    def weight_to_core(other, dy, i):
        part = half_rows(other, dy, (rx, rz)[i])
        n = other * 4 + dy
        send(part, part, wc_ss, wc_rs.at[n], sibling)

    def weight_from_core(other, dy):
        arrive(wfull.at[shard(other, dy), oc], wc_rs.at[other * 4 + dy])

    def weight_to_x(dy, from_hbm=False):
        for j, dev in ((0, xp), (1, xm)):
            part = piece(0, dy, rx, j)
            src = w_hbm.at[c, rx, :, colh[j]] if from_hbm else part
            send(src, part, wx_ss, wx_rs.at[dy], dev)

    def weight_from_x(dy):
        arrive(half_rows(1, dy, rx), wx_rs.at[dy])

    def weight_to_z(other, dy):
        for j in range(2):
            part = piece(other, dy, rx, j)
            send(part, part, wz_ss, wz_rs.at[other * 4 + dy], (zp, zm)[j])

    def weight_from_z(other, dy):
        arrive(half_rows(other, dy, rz), wz_rs.at[other * 4 + dy])
        weight_to_core(other, dy, 1)

    def weight_relay(i):
        for j, k, dev in ((0, 3, yp), (1, 1, ym)):
            part = piece(0, k, (rx, rz)[i], j)
            send(part, part, wy2_ss, wy2_rs.at[i], dev)

    def weight_from_relay(i):
        arrive(half_rows(0, 2, (rx, rz)[i]), wy2_rs.at[i])
        weight_to_core(0, 2, i)

    for d, dev in ((0, yp), (1, ym)):
        send(w_hbm.at[c, rx], half_rows(0, 0, rx), wy_ss, wy_rs.at[d], dev)
    weight_to_x(0, True)

    def moment_copy(j):
        src, dst = ((m1_hbm, m1), (m2_hbm, m2))[j]
        return remote(src, dst.at[y], m_ss.at[j], m_rs.at[j], owner_dev)

    @pl.when(jnp.logical_not(owns))
    def _():
        moment_copy(0).start()
        moment_copy(1).start()

    load_proj.wait()
    load_attn.wait()
    for i in range(2, nz):
        load_cot(i).start()
    reduced[...] = jnp.dot(attn[...], proj[...], preferred_element_type=F32).astype(BF16)

    def core_copy(i):
        return remote(csend.at[i], crecv.at[i], c_ss, c_rs.at[i], sibling)

    def part_step(i, carry):
        load_cot(i).wait()
        cols = pl.ds(pl.multiple_of(i * zrows, 128), zrows)
        part = lax.dot_general(
            cot[:, cols], reduced[...], (((0,), (0,)), ((), ())), preferred_element_type=F32
        ).reshape(2, 2, 2 * rows, -1)
        mine = c == 0
        pown[i] = jnp.where(mine, part[:, 0], part[:, 1])
        csend[i] = jnp.where(mine, part[:, 1], part[:, 0]).astype(BF16)
        core_copy(i).start()
        return carry

    lax.fori_loop(0, nz, part_step, 0)

    for load in (load_w, load_m1, load_m2):
        load.start()

    def core_sum(i, carry):
        core_copy(i).wait_recv()
        total = (pown[i] + crecv[i].astype(F32)).astype(BF16).reshape(4, rows, -1)
        q, e = i // ne, i % ne
        for x_ in range(NX):
            fsend[x_ * oc + q * c, q * oc + x_ * c, e] = total[x_]
        return carry

    lax.fori_loop(0, nz, core_sum, 0)
    for k in (1, 3, 2):
        send(fsend.at[(fme + k) % 4], frecv.at[fme], f_ss, f_rs, fdev[k])

    weight_from_x(0)
    weight_to_z(1, 0)
    weight_to_core(1, 0, 0)
    for d, k in ((0, 3), (1, 1)):
        arrive(half_rows(0, k, rx), wy_rs.at[d])
        weight_to_z(0, k)
    weight_relay(0)
    for k in (3, 1):
        weight_to_core(0, k, 0)

    arrive(frecv.at[pl.ds(0, 3)], f_rs)

    def f_sum(i, carry):
        total = fsend[fme, i].astype(F32)
        for k in (1, 2, 3):
            total += frecv[(fme + k) % 4, i].astype(F32)
        gsend[i] = total.astype(BF16)
        return carry

    lax.fori_loop(0, 4, f_sum, 0)
    for k in (1, 3, 2):
        send(gsend.at[(gme + k) % 4], grecv.at[gme], g_ss, g_rs, gdev[k])

    weight_to_x(3)
    weight_to_x(1)

    weight_from_relay(0)
    weight_to_x(2)

    arrive(grecv.at[pl.ds(0, 3)], g_rs)

    total = gsend[gme].astype(F32)
    for k in (1, 2, 3):
        total += grecv[(gme + k) % 4].astype(F32)
    zsend[...] = total.astype(BF16)

    def z_copy(e):
        z_ = ne * y + e
        return remote(zsend.at[e], zrecv.at[z], z_ss.at[e], z_rs, device(z_, x, c, y))

    for e in range(ne):
        @pl.when(ne * y + e != z)
        def _():
            z_copy(e).start()

    for k in (3, 1):
        weight_from_z(0, k)
    weight_relay(1)
    weight_from_z(1, 0)
    weight_from_x(3)
    weight_to_z(1, 3)
    weight_to_core(1, 3, 0)

    load_w.wait()
    load_m1.wait()
    load_m2.wait()

    mine = low.at[c, fme, gme, z % ne]

    def low_z_copy(k):
        return remote(mine, mine, lz_ss, lz_rs.at[z % ne], zdev[k])

    def moment_back(j, k):
        y_ = (y + k) % NY
        src, dst = ((fm, fm_mine), (sm, sm_mine))[j]
        return remote(src.at[y_], dst, o_ss.at[j], o_rs.at[j], ydev[k])

    @pl.when(owns)
    def _():
        arrive(zrecv.at[pl.ds(0, nz - 1)], z_rs)
        for j, m in enumerate((m1, m2)):
            arrive(m.at[pl.ds(0, 3)], m_rs.at[j])
        projected = zsend[z % ne].astype(F32)
        for k in range(1, nz):
            projected += zrecv[(z + k) % nz].astype(F32)
        projected = projected.reshape(NY, unit, -1)
        first = 0.9 * m1[...] + 0.1 * projected
        second = 0.999 * m2[...] + 0.001 * projected * projected
        steps = jnp.full((1, first.shape[-1]), step_ref[0], jnp.int32).astype(F32)
        first_hat = first / (1.0 - jnp.power(F32(0.9), steps))
        second_hat = second / (1.0 - jnp.power(F32(0.999), steps))
        low_step = first_hat / (jnp.sqrt(second_hat) + 1e-08)
        low[c, fme, gme, z % ne] = low_step.reshape(rows, -1).astype(BF16)
        for k in range(1, nz):
            low_z_copy(k).start()
        fm[...] = first
        sm[...] = second
        fm_mine[...] = fm[y]
        sm_mine[...] = sm[y]
        for j in range(2):
            for k in (1, 2, 3):
                moment_back(j, k).start()

    span = proj_mine.shape[0]
    proj_mine[...] = proj[pl.ds(pl.multiple_of(fs * span, 64), span), :]

    weight_from_x(1)
    weight_to_z(1, 1)
    weight_to_core(1, 1, 0)
    weight_from_relay(1)
    weight_from_x(2)
    weight_to_z(1, 2)
    weight_to_core(1, 2, 0)

    def grad(other, far):
        pair = y // 2
        q = ((1 - xl) if other else xl) * 2 + ((1 - pair) if far else pair)
        w = wfull[pl.ds(2 * q, 2)].reshape(-1, wfull.shape[-1])
        gi[q] = lax.dot_general(
            cot[...], w, (((1,), (1,)), ((), ())), preferred_element_type=F32
        ).astype(BF16)

    for dy in (3, 1):
        weight_from_core(0, dy)
    grad(0, 0)

    for e in range(ne):
        @pl.when(ne * y + e != z)
        def _():
            arrive(low.at[c, fme, gme, e], lz_rs.at[e])

    def low_to_f(k):
        part = low.at[c, fme, (gme + k) % 4]
        for i in (1, 3, 2):
            send(part, part, lf_ss, lf_rs.at[i - 1], fdev[i])

    def low_core(part):
        send(part, part, lc_ss, lc_rs, sibling)

    part = low.at[c, fme, gme]
    for k in (1, 3, 2):
        send(part, part, lg_ss, lg_rs.at[k - 1], gdev[k])
    low_to_f(0)

    weight_from_core(0, 2)
    grad(0, 1)

    for k in (1, 3, 2):
        arrive(low.at[c, fme, (gme + k) % 4], lg_rs.at[3 - k])
        low_to_f(k)
    low_core(low.at[c, fme])

    for dy in (3, 1, 2):
        weight_from_z(1, dy)

    for dy in (0, 3, 1):
        weight_from_core(1, dy)
    grad(1, 0)
    weight_from_core(1, 2)
    grad(1, 1)

    for k in (1, 3, 2):
        part = low.at[c, (fme + k) % 4]
        arrive(part, lf_rs.at[3 - k])
        low_core(part)

    arrive(low.at[oc], lc_rs)

    @pl.when(jnp.logical_not(owns))
    def _():
        arrive(fm_mine, o_rs.at[0])
        arrive(sm_mine, o_rs.at[1])
        moment_copy(0).wait_send()
        moment_copy(1).wait_send()

    @pl.when(owns)
    def _():
        left(zrecv.at[pl.ds(0, nz - 1)], lz_ss)
        for j, m in enumerate((fm, sm)):
            left(m.at[pl.ds(0, 3)], o_ss.at[j])

    for e in range(ne):
        @pl.when(ne * y + e != z)
        def _():
            z_copy(e).wait_send()

    left(csend, c_ss)
    left(fsend.at[pl.ds(0, 3)], f_ss)
    left(gsend.at[pl.ds(0, 3)], g_ss)
    left(low.at[c, fme, pl.ds(0, 3)], lg_ss)
    left(low.at[c, pl.ds(0, 3)], lf_ss)
    left(low.at[c], lc_ss)
    left(wfull.at[0, 0], wy_ss)
    left(wfull.at[0, 0], wy2_ss)
    left(wfull.at[0], wx_ss)
    left(wfull.at[pl.ds(0, 3), 0], wz_ss)
    left(wfull.at[pl.ds(0, 7), 0], wc_ss)


def finish_kernel(gi, low, proj, fm, sm, gi_hbm, ws_hbm, fm_hbm, sm_hbm, ws, gi_sem, ws_sem, m_sem):
    ne = low.shape[3]
    nz = NY * ne
    width = gi.shape[-1]
    copies = [
        pltpu.make_async_copy(gi.at[q], gi_hbm.at[:, pl.ds(q * width, width)], gi_sem.at[q])
        for q in range(4)
    ]
    copies.append(pltpu.make_async_copy(fm, fm_hbm, m_sem.at[0]))
    copies.append(pltpu.make_async_copy(sm, sm_hbm, m_sem.at[1]))
    for copy in copies:
        copy.start()
    zrows = ws.shape[1] // nz

    def ws_copy(i):
        cols = pl.ds(pl.multiple_of(i * zrows, 128), zrows)
        return pltpu.make_async_copy(ws.at[:, cols], ws_hbm.at[:, cols], ws_sem.at[i])

    def ws_step(i, carry):
        cols = pl.ds(pl.multiple_of(i * zrows, 128), zrows)
        q, e = i // ne, i % ne
        rows = []
        for xh in range(2):
            rows += [low[0, 2 * xh + xl, q, e] for xl in range(2)]
            rows += [low[1, q, 2 * xh + xl, e] for xl in range(2)]
        ws[:, cols] = 0.25 * lax.dot_general(
            proj[...], jnp.concatenate(rows, axis=0), (((1,), (1,)), ((), ())),
            preferred_element_type=F32,
        )
        ws_copy(i).start()
        return carry

    lax.fori_loop(0, nz, ws_step, 0)

    def ws_wait(i, carry):
        ws_copy(i).wait()
        return carry

    lax.fori_loop(0, nz, ws_wait, 0)
    for copy in copies:
        copy.wait()


def on_device(nz, attn, cot, w, proj, m1, m2, steps):
    unit, rank = m1.shape
    tokens, inner = attn.shape
    width = cot.shape[1]
    rows = 4 * unit
    ne = nz // NY
    span = w.shape[0]
    q = span // 4
    dma = pltpu.SemaphoreType.DMA
    one = pltpu.SemaphoreType.DMA
    vm = pltpu.VMEM
    any_ = pl.BlockSpec(memory_space=pl.ANY)
    results = pl.pallas_call(
        functools.partial(kernel, nz, unit),
        out_shape=(
            vm((4, tokens, 2 * span), BF16),
            vm((2, 4, 4, ne, rows, rank), BF16),
            vm((span, rank), BF16),
            vm(m1.shape, F32),
            vm(m2.shape, F32),
        ),
        in_specs=[pl.BlockSpec(memory_space=pltpu.HBM)] * 6 + [pl.BlockSpec(memory_space=pltpu.SMEM)],
        out_specs=(pl.BlockSpec(memory_space=vm),) * 5,
        scratch_shapes=[
            vm((tokens, inner), BF16),
            vm((tokens, width), BF16),
            vm((8, 2, 2, q, width), BF16),
            vm((inner, rank), BF16),
            vm((tokens, rank), BF16),
            vm((nz, 2, 2 * rows, rank), F32),
            vm((nz, 2, 2 * rows, rank), BF16),
            vm((nz, 2, 2 * rows, rank), BF16),
            vm((4, 4, ne, rows, rank), BF16),
            vm((4, 4, ne, rows, rank), BF16),
            vm((4, ne, rows, rank), BF16),
            vm((4, ne, rows, rank), BF16),
            vm((ne, rows, rank), BF16),
            vm((nz, rows, rank), BF16),
            vm((NY, unit, rank), F32),
            vm((NY, unit, rank), F32),
            vm((NY, unit, rank), F32),
            vm((NY, unit, rank), F32),
            dma((5,)), dma((nz,)),
            one, dma((nz,)),
            one, one,
            one, one,
            dma((ne,)), one,
            dma((2,)), dma((2,)),
            dma((2,)), dma((2,)),
            one, dma((ne,)),
            one, dma((3,)),
            one, dma((3,)),
            one, one,
            one, dma((2,)),
            one, dma((2,)),
            one, dma((4,)),
            one, dma((8,)),
            one, dma((8,)),
        ],
        compiler_params=pltpu.CompilerParams(
            collective_id=0, has_side_effects=True, vmem_limit_bytes=40 * 2**20
        ),
    )(
        *(
            pltpu.with_memory_space_constraint(a, pltpu.HBM)
            for a in (attn, cot, w.reshape(2, 2, q, width), proj, m1, m2)
        ),
        steps,
    )
    return pl.pallas_call(
        finish_kernel,
        out_shape=(
            jax.ShapeDtypeStruct((tokens, inner), BF16),
            jax.ShapeDtypeStruct((span, width), F32),
            jax.ShapeDtypeStruct(m1.shape, F32),
            jax.ShapeDtypeStruct(m2.shape, F32),
        ),
        in_specs=[pl.BlockSpec(memory_space=vm)] * 5,
        out_specs=(any_,) * 4,
        scratch_shapes=[vm((span, width), F32), dma((4,)), dma((nz,)), dma((2,))],
        compiler_params=pltpu.CompilerParams(vmem_limit_bytes=16 * 2**20),
    )(*(pltpu.with_memory_space_constraint(a, vm) for a in results))


def solution(mesh):
    placed = (
        P(("dp", "fsdp"), None),
        P(("dp", "fsdp"), None),
        P("fsdp", None),
        P(),
        P(("dp", "fsdp"), None),
        P(("dp", "fsdp"), None),
        P(),
    )
    return jax.shard_map(
        functools.partial(on_device, mesh.shape["dp"] // 4),
        mesh=mesh,
        in_specs=placed,
        out_specs=(
            P(("dp", "fsdp"), None),
            P("fsdp", None),
            P(("dp", "fsdp"), None),
            P(("dp", "fsdp"), None),
        ),
        check_vma=False,
    )
```

```python
import functools

import jax
import jax.numpy as jnp
from jax import lax
from jax.experimental import pallas as pl
from jax.experimental.pallas import tpu as pltpu
from jax.sharding import PartitionSpec as P

MESH = pl.DeviceIdType.MESH
F32 = jnp.float32
BF16 = jnp.bfloat16
NX = 4
NY = 4


def kernel(
    nz, unit,
    attn_hbm, cot_hbm, w_hbm, proj_hbm, m1_hbm, m2_hbm, step_ref,
    gi, low, proj_mine, fm_mine, sm_mine,
    attn, cot, wfull, proj, reduced, pown, csend, crecv, fsend, frecv, gsend, grecv, zsend, zrecv,
    m1, m2, fm, sm,
    load_sem, cload_sem,
    c_ss, c_rs, f_ss, f_rs, g_ss, g_rs, z_ss, z_rs, m_ss, m_rs, o_ss, o_rs,
    lz_ss, lz_rs, lg_ss, lg_rs, lf_ss, lf_rs, lc_ss, lc_rs,
    wy_ss, wy_rs, wy2_ss, wy2_rs, wf_ss, wf_rs, wx_ss, wx_rs, wz_ss, wz_rs, wc_ss, wc_rs,
):
    rows = 4 * unit
    zrows = 8 * rows
    ne = nz // NY
    dp, fs = lax.axis_index("dp"), lax.axis_index("fsdp")
    z, xh, c = dp // 4, (dp // 2) % 2, dp % 2
    xl, y = fs // NY, fs % NY
    x = xh * 2 + xl
    oc = 1 - c
    fme = x * oc + y * c
    gme = y * oc + x * c
    owner = z // ne
    owns = y == owner

    def device(z_, x_, c_, y_):
        return (z_ * 4 + (x_ // 2) * 2 + c_, (x_ % 2) * NY + y_)

    sibling = device(z, x, oc, y)
    xdev = [None] + [device(z, (x + k) % NX, c, y) for k in (1, 2, 3)]
    ydev = [None] + [device(z, x, c, (y + k) % NY) for k in (1, 2, 3)]
    zdev = [None] + [device((z + k) % nz, x, c, y) for k in range(1, nz)]
    fdev = [None] + [device(z, (x + k * oc) % NX, c, (y + k * c) % NY) for k in (1, 2, 3)]
    gdev = [None] + [device(z, (x + k * c) % NX, c, (y + k * oc) % NY) for k in (1, 2, 3)]
    owner_dev = device(z, x, c, owner)

    def remote(src, dst, ss, rs, dev):
        return pltpu.make_async_remote_copy(
            src_ref=src, dst_ref=dst, send_sem=ss, recv_sem=rs, device_id=dev, device_id_type=MESH
        )

    def send(*args):
        remote(*args).start()

    def arrive(part, rs):
        remote(part, part, rs, rs, sibling).wait_recv()

    def left(part, ss):
        remote(part, part, ss, ss, sibling).wait_send()

    load_proj = pltpu.make_async_copy(proj_hbm, proj, load_sem.at[0])
    load_attn = pltpu.make_async_copy(attn_hbm, attn, load_sem.at[1])
    load_proj.start()
    load_attn.start()

    def load_cot(i):
        cols = pl.ds(pl.multiple_of(i * zrows, 128), zrows)
        return pltpu.make_async_copy(cot_hbm.at[:, cols], cot.at[:, cols], cload_sem.at[i])

    load_cot(0).start()
    load_cot(1).start()
    own = xl * NY + y
    load_w = pltpu.make_async_copy(w_hbm, wfull.at[own], load_sem.at[2])
    load_m1 = pltpu.make_async_copy(m1_hbm, m1.at[y], load_sem.at[3])
    load_m2 = pltpu.make_async_copy(m2_hbm, m2.at[y], load_sem.at[4])

    barrier = pltpu.get_barrier_semaphore()
    partners = [sibling] + xdev[1:] + ydev[1:] + zdev[1:]
    for dev in partners:
        pl.semaphore_signal(barrier, inc=1, device_id=dev, device_id_type=MESH)
    pl.semaphore_wait(barrier, len(partners))

    yp, ym, xp, xm, zp, zm = ydev[1], ydev[3], xdev[1], xdev[3], zdev[1], zdev[nz - 1]
    rx = z % 2
    rz = 1 - rx
    hcol = w_hbm.shape[-1] // 2
    colh = [pl.ds(0, hcol), pl.ds(hcol, hcol)]

    def shard(other, dy):
        return ((1 - xl) if other else xl) * NY + (y + dy) % NY

    def half_rows(other, dy, r):
        return wfull.at[shard(other, dy), c, r]

    def piece(other, dy, r, j):
        return wfull.at[shard(other, dy), c, r, :, colh[j]]

    def weight_to_core(other, dy, i):
        part = half_rows(other, dy, (rx, rz)[i])
        n = other * 4 + dy
        send(part, part, wc_ss, wc_rs.at[n], sibling)

    def weight_from_core(other, dy):
        arrive(wfull.at[shard(other, dy), oc], wc_rs.at[other * 4 + dy])

    def weight_to_x(dy, i, from_hbm=False):
        r = (rx, rz)[i]
        for j, dev in ((0, xp), (1, xm)):
            part = piece(0, dy, r, j)
            src = w_hbm.at[c, r, :, colh[j]] if from_hbm else part
            send(src, part, wx_ss, wx_rs.at[dy + 4 * i], dev)

    def weight_from_x(dy, i):
        arrive(half_rows(1, dy, (rx, rz)[i]), wx_rs.at[dy + 4 * i])
        weight_to_core(1, dy, i)

    def weight_far_to_y():
        part = half_rows(1, 0, rz)
        for d, dev in ((0, yp), (1, ym)):
            send(part, part, wf_ss, wf_rs.at[d], dev)

    def weight_far_from_y():
        for d, k in ((0, 3), (1, 1)):
            arrive(half_rows(1, k, rz), wf_rs.at[d])
            weight_to_core(1, k, 1)

    def weight_to_z(other, dy):
        for j in range(2):
            part = piece(other, dy, rx, j)
            send(part, part, wz_ss, wz_rs.at[other * 4 + dy], (zp, zm)[j])

    def weight_from_z(other, dy):
        arrive(half_rows(other, dy, rz), wz_rs.at[other * 4 + dy])
        weight_to_core(other, dy, 1)

    def weight_relay(i):
        for j, k, dev in ((0, 3, yp), (1, 1, ym)):
            part = piece(0, k, (rx, rz)[i], j)
            send(part, part, wy2_ss, wy2_rs.at[i], dev)

    def weight_from_relay(i):
        arrive(half_rows(0, 2, (rx, rz)[i]), wy2_rs.at[i])
        weight_to_core(0, 2, i)

    for d, dev in ((0, yp), (1, ym)):
        send(w_hbm.at[c, rx], half_rows(0, 0, rx), wy_ss, wy_rs.at[d], dev)
    weight_to_x(0, 0, True)

    def moment_copy(j):
        src, dst = ((m1_hbm, m1), (m2_hbm, m2))[j]
        return remote(src, dst.at[y], m_ss.at[j], m_rs.at[j], owner_dev)

    @pl.when(jnp.logical_not(owns))
    def _():
        moment_copy(0).start()
        moment_copy(1).start()

    load_proj.wait()
    load_attn.wait()
    for i in range(2, nz):
        load_cot(i).start()
    reduced[...] = jnp.dot(attn[...], proj[...], preferred_element_type=F32).astype(BF16)

    def core_copy(i):
        return remote(csend.at[i], crecv.at[i], c_ss, c_rs.at[i], sibling)

    def part_step(i, carry):
        load_cot(i).wait()
        cols = pl.ds(pl.multiple_of(i * zrows, 128), zrows)
        part = lax.dot_general(
            cot[:, cols], reduced[...], (((0,), (0,)), ((), ())), preferred_element_type=F32
        ).reshape(2, 2, 2 * rows, -1)
        mine = c == 0
        pown[i] = jnp.where(mine, part[:, 0], part[:, 1])
        csend[i] = jnp.where(mine, part[:, 1], part[:, 0]).astype(BF16)
        core_copy(i).start()
        return carry

    lax.fori_loop(0, nz, part_step, 0)

    for load in (load_w, load_m1, load_m2):
        load.start()

    def core_sum(i, carry):
        core_copy(i).wait_recv()
        total = (pown[i] + crecv[i].astype(F32)).astype(BF16).reshape(4, rows, -1)
        q, e = i // ne, i % ne
        for x_ in range(NX):
            fsend[x_ * oc + q * c, q * oc + x_ * c, e] = total[x_]
        return carry

    lax.fori_loop(0, nz, core_sum, 0)
    for k in (1, 3, 2):
        send(fsend.at[(fme + k) % 4], frecv.at[fme], f_ss, f_rs, fdev[k])

    weight_from_x(0, 0)
    weight_to_z(1, 0)
    for d, k in ((0, 3), (1, 1)):
        arrive(half_rows(0, k, rx), wy_rs.at[d])
        weight_to_z(0, k)
    for k in (3, 1):
        weight_to_core(0, k, 0)

    arrive(frecv.at[pl.ds(0, 3)], f_rs)

    def f_sum(i, carry):
        total = fsend[fme, i].astype(F32)
        for k in (1, 2, 3):
            total += frecv[(fme + k) % 4, i].astype(F32)
        gsend[i] = total.astype(BF16)
        return carry

    lax.fori_loop(0, 4, f_sum, 0)
    for k in (1, 3, 2):
        send(gsend.at[(gme + k) % 4], grecv.at[gme], g_ss, g_rs, gdev[k])

    weight_relay(0)
    weight_to_x(3, 0)
    weight_from_z(1, 0)
    weight_far_to_y()

    arrive(grecv.at[pl.ds(0, 3)], g_rs)

    total = gsend[gme].astype(F32)
    for k in (1, 2, 3):
        total += grecv[(gme + k) % 4].astype(F32)
    zsend[...] = total.astype(BF16)

    def z_copy(e):
        z_ = ne * y + e
        return remote(zsend.at[e], zrecv.at[z], z_ss.at[e], z_rs, device(z_, x, c, y))

    for e in range(ne):
        @pl.when(ne * y + e != z)
        def _():
            z_copy(e).start()

    weight_to_x(1, 0)
    weight_from_relay(0)
    weight_to_x(2, 0)

    for k in (3, 1):
        weight_from_z(0, k)
    weight_relay(1)

    load_w.wait()
    load_m1.wait()
    load_m2.wait()

    mine = low.at[c, fme, gme, z % ne]

    def low_z_copy(k):
        return remote(mine, mine, lz_ss, lz_rs.at[z % ne], zdev[k])

    def moment_back(j, k):
        y_ = (y + k) % NY
        src, dst = ((fm, fm_mine), (sm, sm_mine))[j]
        return remote(src.at[y_], dst, o_ss.at[j], o_rs.at[j], ydev[k])

    @pl.when(owns)
    def _():
        arrive(zrecv.at[pl.ds(0, nz - 1)], z_rs)
        for j, m in enumerate((m1, m2)):
            arrive(m.at[pl.ds(0, 3)], m_rs.at[j])
        projected = zsend[z % ne].astype(F32)
        for k in range(1, nz):
            projected += zrecv[(z + k) % nz].astype(F32)
        projected = projected.reshape(NY, unit, -1)
        first = 0.9 * m1[...] + 0.1 * projected
        second = 0.999 * m2[...] + 0.001 * projected * projected
        steps = jnp.full((1, first.shape[-1]), step_ref[0], jnp.int32).astype(F32)
        first_hat = first / (1.0 - jnp.power(F32(0.9), steps))
        second_hat = second / (1.0 - jnp.power(F32(0.999), steps))
        low_step = first_hat / (jnp.sqrt(second_hat) + 1e-08)
        low[c, fme, gme, z % ne] = low_step.reshape(rows, -1).astype(BF16)
        for k in range(1, nz):
            low_z_copy(k).start()
        fm[...] = first
        sm[...] = second
        fm_mine[...] = fm[y]
        sm_mine[...] = sm[y]
        for j in range(2):
            for k in (1, 2, 3):
                moment_back(j, k).start()

    span = proj_mine.shape[0]
    proj_mine[...] = proj[pl.ds(pl.multiple_of(fs * span, 64), span), :]

    def grad(other, far):
        pair = y // 2
        q = ((1 - xl) if other else xl) * 2 + ((1 - pair) if far else pair)
        w = wfull[pl.ds(2 * q, 2)].reshape(-1, wfull.shape[-1])
        gi[q] = lax.dot_general(
            cot[...], w, (((1,), (1,)), ((), ())), preferred_element_type=F32
        ).astype(BF16)

    for dy in (3, 1):
        weight_from_core(0, dy)
    grad(0, 0)

    for dy in (3, 1):
        weight_from_x(dy, 0)

    for e in range(ne):
        @pl.when(ne * y + e != z)
        def _():
            arrive(low.at[c, fme, gme, e], lz_rs.at[e])

    def low_to_f(k):
        part = low.at[c, fme, (gme + k) % 4]
        for i in (1, 3, 2):
            send(part, part, lf_ss, lf_rs.at[i - 1], fdev[i])

    def low_core(part):
        send(part, part, lc_ss, lc_rs, sibling)

    part = low.at[c, fme, gme]
    for k in (1, 3, 2):
        send(part, part, lg_ss, lg_rs.at[k - 1], gdev[k])
    low_to_f(0)

    weight_from_relay(1)
    weight_to_x(2, 1)
    weight_from_x(2, 0)
    weight_far_from_y()

    weight_from_core(0, 2)
    grad(0, 1)

    for k in (1, 3, 2):
        arrive(low.at[c, fme, (gme + k) % 4], lg_rs.at[3 - k])
        low_to_f(k)
    low_core(low.at[c, fme])

    weight_from_x(2, 1)

    for dy in (0, 3, 1):
        weight_from_core(1, dy)
    grad(1, 0)
    weight_from_core(1, 2)
    grad(1, 1)

    for k in (1, 3, 2):
        part = low.at[c, (fme + k) % 4]
        arrive(part, lf_rs.at[3 - k])
        low_core(part)

    arrive(low.at[oc], lc_rs)

    @pl.when(jnp.logical_not(owns))
    def _():
        arrive(fm_mine, o_rs.at[0])
        arrive(sm_mine, o_rs.at[1])
        moment_copy(0).wait_send()
        moment_copy(1).wait_send()

    @pl.when(owns)
    def _():
        left(zrecv.at[pl.ds(0, nz - 1)], lz_ss)
        for j, m in enumerate((fm, sm)):
            left(m.at[pl.ds(0, 3)], o_ss.at[j])

    for e in range(ne):
        @pl.when(ne * y + e != z)
        def _():
            z_copy(e).wait_send()

    left(csend, c_ss)
    left(fsend.at[pl.ds(0, 3)], f_ss)
    left(gsend.at[pl.ds(0, 3)], g_ss)
    left(low.at[c, fme, pl.ds(0, 3)], lg_ss)
    left(low.at[c, pl.ds(0, 3)], lf_ss)
    left(low.at[c], lc_ss)
    left(wfull.at[0, 0], wy_ss)
    left(wfull.at[0, 0], wy2_ss)
    left(wfull.at[0, 0], wf_ss)
    left(wfull.at[pl.ds(0, 5), 0, 0], wx_ss)
    left(wfull.at[pl.ds(0, 3), 0, 0], wz_ss)
    left(wfull.at[pl.ds(0, 7), 0], wc_ss)


def finish_kernel(gi, low, proj, fm, sm, gi_hbm, ws_hbm, fm_hbm, sm_hbm, ws, gi_sem, ws_sem, m_sem):
    ne = low.shape[3]
    nz = NY * ne
    width = gi.shape[-1]
    copies = [
        pltpu.make_async_copy(gi.at[q], gi_hbm.at[:, pl.ds(q * width, width)], gi_sem.at[q])
        for q in range(4)
    ]
    copies.append(pltpu.make_async_copy(fm, fm_hbm, m_sem.at[0]))
    copies.append(pltpu.make_async_copy(sm, sm_hbm, m_sem.at[1]))
    for copy in copies:
        copy.start()
    zrows = ws.shape[1] // nz

    def ws_copy(i):
        cols = pl.ds(pl.multiple_of(i * 2 * zrows, 128), 2 * zrows)
        return pltpu.make_async_copy(ws.at[:, cols], ws_hbm.at[:, cols], ws_sem.at[i])

    def ws_step(i, carry):
        for n in range(2):
            t = 2 * i + n
            q, e = t // ne, t % ne
            rows = []
            for xh in range(2):
                rows += [low[0, 2 * xh + xl, q, e] for xl in range(2)]
                rows += [low[1, q, 2 * xh + xl, e] for xl in range(2)]
            ws[:, pl.ds(pl.multiple_of(t * zrows, 128), zrows)] = 0.25 * lax.dot_general(
                proj[...], jnp.concatenate(rows, axis=0), (((1,), (1,)), ((), ())),
                preferred_element_type=F32,
            )
        ws_copy(i).start()
        return carry

    lax.fori_loop(0, nz // 2, ws_step, 0)

    def ws_wait(i, carry):
        ws_copy(i).wait()
        return carry

    lax.fori_loop(0, nz // 2, ws_wait, 0)
    for copy in copies:
        copy.wait()


def on_device(nz, attn, cot, w, proj, m1, m2, steps):
    unit, rank = m1.shape
    tokens, inner = attn.shape
    width = cot.shape[1]
    rows = 4 * unit
    ne = nz // NY
    span = w.shape[0]
    q = span // 4
    dma = pltpu.SemaphoreType.DMA
    one = pltpu.SemaphoreType.DMA
    vm = pltpu.VMEM
    any_ = pl.BlockSpec(memory_space=pl.ANY)
    results = pl.pallas_call(
        functools.partial(kernel, nz, unit),
        out_shape=(
            vm((4, tokens, 2 * span), BF16),
            vm((2, 4, 4, ne, rows, rank), BF16),
            vm((span, rank), BF16),
            vm(m1.shape, F32),
            vm(m2.shape, F32),
        ),
        in_specs=[pl.BlockSpec(memory_space=pltpu.HBM)] * 6 + [pl.BlockSpec(memory_space=pltpu.SMEM)],
        out_specs=(pl.BlockSpec(memory_space=vm),) * 5,
        scratch_shapes=[
            vm((tokens, inner), BF16),
            vm((tokens, width), BF16),
            vm((8, 2, 2, q, width), BF16),
            vm((inner, rank), BF16),
            vm((tokens, rank), BF16),
            vm((nz, 2, 2 * rows, rank), F32),
            vm((nz, 2, 2 * rows, rank), BF16),
            vm((nz, 2, 2 * rows, rank), BF16),
            vm((4, 4, ne, rows, rank), BF16),
            vm((4, 4, ne, rows, rank), BF16),
            vm((4, ne, rows, rank), BF16),
            vm((4, ne, rows, rank), BF16),
            vm((ne, rows, rank), BF16),
            vm((nz, rows, rank), BF16),
            vm((NY, unit, rank), F32),
            vm((NY, unit, rank), F32),
            vm((NY, unit, rank), F32),
            vm((NY, unit, rank), F32),
            dma((5,)), dma((nz,)),
            one, dma((nz,)),
            one, one,
            one, one,
            dma((ne,)), one,
            dma((2,)), dma((2,)),
            dma((2,)), dma((2,)),
            one, dma((ne,)),
            one, dma((3,)),
            one, dma((3,)),
            one, one,
            one, dma((2,)),
            one, dma((2,)),
            one, dma((2,)),
            one, dma((8,)),
            one, dma((8,)),
            one, dma((8,)),
        ],
        compiler_params=pltpu.CompilerParams(
            collective_id=0, has_side_effects=True, vmem_limit_bytes=40 * 2**20
        ),
    )(
        *(
            pltpu.with_memory_space_constraint(a, pltpu.HBM)
            for a in (attn, cot, w.reshape(2, 2, q, width), proj, m1, m2)
        ),
        steps,
    )
    return pl.pallas_call(
        finish_kernel,
        out_shape=(
            jax.ShapeDtypeStruct((tokens, inner), BF16),
            jax.ShapeDtypeStruct((span, width), F32),
            jax.ShapeDtypeStruct(m1.shape, F32),
            jax.ShapeDtypeStruct(m2.shape, F32),
        ),
        in_specs=[pl.BlockSpec(memory_space=vm)] * 5,
        out_specs=(any_,) * 4,
        scratch_shapes=[vm((span, width), F32), dma((4,)), dma((nz // 2,)), dma((2,))],
        compiler_params=pltpu.CompilerParams(vmem_limit_bytes=16 * 2**20),
    )(*(pltpu.with_memory_space_constraint(a, vm) for a in results))


def solution(mesh):
    placed = (
        P(("dp", "fsdp"), None),
        P(("dp", "fsdp"), None),
        P("fsdp", None),
        P(),
        P(("dp", "fsdp"), None),
        P(("dp", "fsdp"), None),
        P(),
    )
    return jax.shard_map(
        functools.partial(on_device, mesh.shape["dp"] // 4),
        mesh=mesh,
        in_specs=placed,
        out_specs=(
            P(("dp", "fsdp"), None),
            P("fsdp", None),
            P(("dp", "fsdp"), None),
            P(("dp", "fsdp"), None),
        ),
        check_vma=False,
    )
```

```python
import functools

import jax
import jax.numpy as jnp
from jax import lax
from jax.experimental import pallas as pl
from jax.experimental.pallas import tpu as pltpu
from jax.sharding import PartitionSpec as P

MESH = pl.DeviceIdType.MESH
F32 = jnp.float32
BF16 = jnp.bfloat16
NX = 4
NY = 4


def kernel(
    nz, unit,
    attn_hbm, cot_hbm, w_hbm, proj_hbm, m1_hbm, m2_hbm, step_ref,
    gi, low, proj_mine, fm_mine, sm_mine,
    attn, cot, wfull, proj, reduced, pown, csend, crecv, fsend, frecv, gsend, grecv, zsend, zrecv,
    m1, m2, fm, sm,
    load_sem, cload_sem,
    c_ss, c_rs, f_ss, f_rs, g_ss, g_rs, z_ss, z_rs, m_ss, m_rs, o_ss, o_rs,
    lz_ss, lz_rs, lg_ss, lg_rs, lf_ss, lf_rs, lc_ss, lc_rs,
    wy_ss, wy_rs, wy2_ss, wy2_rs, wf_ss, wf_rs, wx_ss, wx_rs, wz_ss, wz_rs, wc_ss, wc_rs,
):
    rows = 4 * unit
    zrows = 8 * rows
    ne = nz // NY
    dp, fs = lax.axis_index("dp"), lax.axis_index("fsdp")
    z, xh, c = dp // 4, (dp // 2) % 2, dp % 2
    xl, y = fs // NY, fs % NY
    x = xh * 2 + xl
    oc = 1 - c
    fme = x * oc + y * c
    gme = y * oc + x * c
    owner = z // ne
    owns = y == owner

    def device(z_, x_, c_, y_):
        return (z_ * 4 + (x_ // 2) * 2 + c_, (x_ % 2) * NY + y_)

    sibling = device(z, x, oc, y)
    xdev = [None] + [device(z, (x + k) % NX, c, y) for k in (1, 2, 3)]
    ydev = [None] + [device(z, x, c, (y + k) % NY) for k in (1, 2, 3)]
    zdev = [None] + [device((z + k) % nz, x, c, y) for k in range(1, nz)]
    fdev = [None] + [device(z, (x + k * oc) % NX, c, (y + k * c) % NY) for k in (1, 2, 3)]
    gdev = [None] + [device(z, (x + k * c) % NX, c, (y + k * oc) % NY) for k in (1, 2, 3)]
    owner_dev = device(z, x, c, owner)

    def remote(src, dst, ss, rs, dev):
        return pltpu.make_async_remote_copy(
            src_ref=src, dst_ref=dst, send_sem=ss, recv_sem=rs, device_id=dev, device_id_type=MESH
        )

    def send(*args):
        remote(*args).start()

    def arrive(part, rs):
        remote(part, part, rs, rs, sibling).wait_recv()

    def left(part, ss):
        remote(part, part, ss, ss, sibling).wait_send()

    load_proj = pltpu.make_async_copy(proj_hbm, proj, load_sem.at[0])
    load_attn = pltpu.make_async_copy(attn_hbm, attn, load_sem.at[1])
    load_proj.start()
    load_attn.start()

    def load_cot(i):
        cols = pl.ds(pl.multiple_of(i * zrows, 128), zrows)
        return pltpu.make_async_copy(cot_hbm.at[:, cols], cot.at[:, cols], cload_sem.at[i])

    load_cot(0).start()
    load_cot(1).start()
    own = xl * NY + y
    load_w = pltpu.make_async_copy(w_hbm, wfull.at[own], load_sem.at[2])
    load_m1 = pltpu.make_async_copy(m1_hbm, m1.at[y], load_sem.at[3])
    load_m2 = pltpu.make_async_copy(m2_hbm, m2.at[y], load_sem.at[4])

    barrier = pltpu.get_barrier_semaphore()
    partners = [sibling] + xdev[1:] + ydev[1:] + zdev[1:]
    for dev in partners:
        pl.semaphore_signal(barrier, inc=1, device_id=dev, device_id_type=MESH)
    pl.semaphore_wait(barrier, len(partners))

    yp, ym, xp, xm, zp, zm = ydev[1], ydev[3], xdev[1], xdev[3], zdev[1], zdev[nz - 1]
    rx = z % 2
    rz = 1 - rx
    hcol = w_hbm.shape[-1] // 2
    colh = [pl.ds(0, hcol), pl.ds(hcol, hcol)]

    def shard(other, dy):
        return ((1 - xl) if other else xl) * NY + (y + dy) % NY

    def half_rows(other, dy, r):
        return wfull.at[shard(other, dy), c, r]

    def piece(other, dy, r, j):
        return wfull.at[shard(other, dy), c, r, :, colh[j]]

    def weight_to_core(other, dy, i):
        part = half_rows(other, dy, (rx, rz)[i])
        n = other * 4 + dy
        send(part, part, wc_ss, wc_rs.at[n], sibling)

    def weight_from_core(other, dy):
        arrive(wfull.at[shard(other, dy), oc], wc_rs.at[other * 4 + dy])

    def weight_to_x(dy, i, from_hbm=False):
        r = (rx, rz)[i]
        for j, dev in ((0, xp), (1, xm)):
            part = piece(0, dy, r, j)
            src = w_hbm.at[c, r, :, colh[j]] if from_hbm else part
            send(src, part, wx_ss, wx_rs.at[dy + 4 * i], dev)

    def weight_from_x(dy, i):
        arrive(half_rows(1, dy, (rx, rz)[i]), wx_rs.at[dy + 4 * i])
        weight_to_core(1, dy, i)

    def weight_far_to_y(j):
        part = piece(1, 0, rz, j)
        for dev in (yp, ym):
            send(part, part, wf_ss, wf_rs.at[j], dev)

    def weight_far_from_y():
        for j in range(2):
            arrive(half_rows(1, 0, rz), wf_rs.at[j])
        for k in (3, 1):
            weight_to_core(1, k, 1)

    def weight_to_z(other, dy):
        for j in range(2):
            part = piece(other, dy, rx, j)
            send(part, part, wz_ss, wz_rs.at[other * 4 + dy], (zp, zm)[j])

    def weight_from_z(other, dy):
        arrive(half_rows(other, dy, rz), wz_rs.at[other * 4 + dy])
        weight_to_core(other, dy, 1)

    def weight_relay(i):
        for j, k, dev in ((0, 3, yp), (1, 1, ym)):
            part = piece(0, k, (rx, rz)[i], j)
            send(part, part, wy2_ss, wy2_rs.at[i], dev)

    def weight_from_relay(i):
        arrive(half_rows(0, 2, (rx, rz)[i]), wy2_rs.at[i])
        weight_to_core(0, 2, i)

    for d, dev in ((0, yp), (1, ym)):
        send(w_hbm.at[c, rx], half_rows(0, 0, rx), wy_ss, wy_rs.at[d], dev)
    weight_to_x(0, 0, True)

    def moment_copy(j):
        src, dst = ((m1_hbm, m1), (m2_hbm, m2))[j]
        return remote(src, dst.at[y], m_ss.at[j], m_rs.at[j], owner_dev)

    @pl.when(jnp.logical_not(owns))
    def _():
        moment_copy(0).start()
        moment_copy(1).start()

    load_proj.wait()
    load_attn.wait()
    for i in range(2, nz):
        load_cot(i).start()
    reduced[...] = jnp.dot(attn[...], proj[...], preferred_element_type=F32).astype(BF16)

    def core_copy(i):
        return remote(csend.at[i], crecv.at[i], c_ss, c_rs.at[i], sibling)

    def part_step(i, carry):
        load_cot(i).wait()
        cols = pl.ds(pl.multiple_of(i * zrows, 128), zrows)
        part = lax.dot_general(
            cot[:, cols], reduced[...], (((0,), (0,)), ((), ())), preferred_element_type=F32
        ).reshape(2, 2, 2 * rows, -1)
        mine = c == 0
        pown[i] = jnp.where(mine, part[:, 0], part[:, 1])
        csend[i] = jnp.where(mine, part[:, 1], part[:, 0]).astype(BF16)
        core_copy(i).start()
        return carry

    lax.fori_loop(0, nz, part_step, 0)

    for load in (load_w, load_m1, load_m2):
        load.start()

    def core_sum(i, carry):
        core_copy(i).wait_recv()
        total = (pown[i] + crecv[i].astype(F32)).astype(BF16).reshape(4, rows, -1)
        q, e = i // ne, i % ne
        for x_ in range(NX):
            fsend[x_ * oc + q * c, q * oc + x_ * c, e] = total[x_]
        return carry

    lax.fori_loop(0, nz, core_sum, 0)
    for k in (1, 3, 2):
        send(fsend.at[(fme + k) % 4], frecv.at[fme], f_ss, f_rs, fdev[k])

    weight_from_x(0, 0)
    weight_to_z(1, 0)
    for d, k in ((0, 3), (1, 1)):
        arrive(half_rows(0, k, rx), wy_rs.at[d])
        weight_to_z(0, k)
    for k in (3, 1):
        weight_to_core(0, k, 0)

    arrive(frecv.at[pl.ds(0, 3)], f_rs)

    def f_sum(i, carry):
        total = fsend[fme, i].astype(F32)
        for k in (1, 2, 3):
            total += frecv[(fme + k) % 4, i].astype(F32)
        gsend[i] = total.astype(BF16)
        return carry

    lax.fori_loop(0, 4, f_sum, 0)
    for k in (1, 3, 2):
        send(gsend.at[(gme + k) % 4], grecv.at[gme], g_ss, g_rs, gdev[k])

    weight_relay(0)
    weight_to_x(3, 0)
    weight_from_z(1, 0)
    weight_far_to_y(0)

    arrive(grecv.at[pl.ds(0, 3)], g_rs)

    total = gsend[gme].astype(F32)
    for k in (1, 2, 3):
        total += grecv[(gme + k) % 4].astype(F32)
    zsend[...] = total.astype(BF16)

    def z_copy(e):
        z_ = ne * y + e
        return remote(zsend.at[e], zrecv.at[z], z_ss.at[e], z_rs, device(z_, x, c, y))

    for e in range(ne):
        @pl.when(ne * y + e != z)
        def _():
            z_copy(e).start()

    weight_to_x(1, 0)
    weight_from_relay(0)
    weight_to_x(2, 0)

    for k in (3, 1):
        weight_from_z(0, k)
    weight_relay(1)
    weight_far_to_y(1)

    load_w.wait()
    load_m1.wait()
    load_m2.wait()

    mine = low.at[c, fme, gme, z % ne]

    def low_z_copy(k):
        return remote(mine, mine, lz_ss, lz_rs.at[z % ne], zdev[k])

    def moment_back(j, k):
        y_ = (y + k) % NY
        src, dst = ((fm, fm_mine), (sm, sm_mine))[j]
        return remote(src.at[y_], dst, o_ss.at[j], o_rs.at[j], ydev[k])

    @pl.when(owns)
    def _():
        arrive(zrecv.at[pl.ds(0, nz - 1)], z_rs)
        for j, m in enumerate((m1, m2)):
            arrive(m.at[pl.ds(0, 3)], m_rs.at[j])
        projected = zsend[z % ne].astype(F32)
        for k in range(1, nz):
            projected += zrecv[(z + k) % nz].astype(F32)
        projected = projected.reshape(NY, unit, -1)
        first = 0.9 * m1[...] + 0.1 * projected
        second = 0.999 * m2[...] + 0.001 * projected * projected
        steps = jnp.full((1, first.shape[-1]), step_ref[0], jnp.int32).astype(F32)
        first_hat = first / (1.0 - jnp.power(F32(0.9), steps))
        second_hat = second / (1.0 - jnp.power(F32(0.999), steps))
        low_step = first_hat / (jnp.sqrt(second_hat) + 1e-08)
        low[c, fme, gme, z % ne] = low_step.reshape(rows, -1).astype(BF16)
        for k in range(1, nz):
            low_z_copy(k).start()
        fm[...] = first
        sm[...] = second
        fm_mine[...] = fm[y]
        sm_mine[...] = sm[y]
        for j in range(2):
            for k in (1, 2, 3):
                moment_back(j, k).start()

    span = proj_mine.shape[0]
    proj_mine[...] = proj[pl.ds(pl.multiple_of(fs * span, 64), span), :]

    def grad(other, far):
        pair = y // 2
        q = ((1 - xl) if other else xl) * 2 + ((1 - pair) if far else pair)
        w = wfull[pl.ds(2 * q, 2)].reshape(-1, wfull.shape[-1])
        gi[q] = lax.dot_general(
            cot[...], w, (((1,), (1,)), ((), ())), preferred_element_type=F32
        ).astype(BF16)

    for dy in (3, 1):
        weight_from_core(0, dy)
    grad(0, 0)

    weight_from_relay(1)
    weight_to_x(2, 1)
    for dy in (3, 1):
        weight_from_x(dy, 0)

    for e in range(ne):
        @pl.when(ne * y + e != z)
        def _():
            arrive(low.at[c, fme, gme, e], lz_rs.at[e])

    def low_to_f(k):
        part = low.at[c, fme, (gme + k) % 4]
        for i in (1, 3, 2):
            send(part, part, lf_ss, lf_rs.at[i - 1], fdev[i])

    def low_core(part):
        send(part, part, lc_ss, lc_rs, sibling)

    part = low.at[c, fme, gme]
    for k in (1, 3, 2):
        send(part, part, lg_ss, lg_rs.at[k - 1], gdev[k])
    low_to_f(0)

    weight_from_x(2, 0)
    weight_far_from_y()

    weight_from_core(0, 2)
    grad(0, 1)

    for k in (1, 3, 2):
        arrive(low.at[c, fme, (gme + k) % 4], lg_rs.at[3 - k])
        low_to_f(k)
    low_core(low.at[c, fme])

    weight_from_x(2, 1)

    for dy in (0, 3, 1):
        weight_from_core(1, dy)
    grad(1, 0)
    weight_from_core(1, 2)
    grad(1, 1)

    for k in (1, 3, 2):
        part = low.at[c, (fme + k) % 4]
        arrive(part, lf_rs.at[3 - k])
        low_core(part)

    arrive(low.at[oc], lc_rs)

    @pl.when(jnp.logical_not(owns))
    def _():
        arrive(fm_mine, o_rs.at[0])
        arrive(sm_mine, o_rs.at[1])
        moment_copy(0).wait_send()
        moment_copy(1).wait_send()

    @pl.when(owns)
    def _():
        left(zrecv.at[pl.ds(0, nz - 1)], lz_ss)
        for j, m in enumerate((fm, sm)):
            left(m.at[pl.ds(0, 3)], o_ss.at[j])

    for e in range(ne):
        @pl.when(ne * y + e != z)
        def _():
            z_copy(e).wait_send()

    left(csend, c_ss)
    left(fsend.at[pl.ds(0, 3)], f_ss)
    left(gsend.at[pl.ds(0, 3)], g_ss)
    left(low.at[c, fme, pl.ds(0, 3)], lg_ss)
    left(low.at[c, pl.ds(0, 3)], lf_ss)
    left(low.at[c], lc_ss)
    left(wfull.at[0, 0], wy_ss)
    left(wfull.at[0, 0], wy2_ss)
    left(wfull.at[0, 0], wf_ss)
    left(wfull.at[pl.ds(0, 5), 0, 0], wx_ss)
    left(wfull.at[pl.ds(0, 3), 0, 0], wz_ss)
    left(wfull.at[pl.ds(0, 7), 0], wc_ss)


def finish_kernel(gi, low, proj, fm, sm, gi_hbm, ws_hbm, fm_hbm, sm_hbm, ws, gi_sem, ws_sem, m_sem):
    ne = low.shape[3]
    nz = NY * ne
    width = gi.shape[-1]
    copies = [
        pltpu.make_async_copy(gi.at[q], gi_hbm.at[:, pl.ds(q * width, width)], gi_sem.at[q])
        for q in range(4)
    ]
    copies.append(pltpu.make_async_copy(fm, fm_hbm, m_sem.at[0]))
    copies.append(pltpu.make_async_copy(sm, sm_hbm, m_sem.at[1]))
    for copy in copies:
        copy.start()
    zrows = ws.shape[1] // nz

    def ws_copy(i):
        cols = pl.ds(pl.multiple_of(i * 2 * zrows, 128), 2 * zrows)
        return pltpu.make_async_copy(ws.at[:, cols], ws_hbm.at[:, cols], ws_sem.at[i])

    def ws_step(i, carry):
        for n in range(2):
            t = 2 * i + n
            q, e = t // ne, t % ne
            rows = []
            for xh in range(2):
                rows += [low[0, 2 * xh + xl, q, e] for xl in range(2)]
                rows += [low[1, q, 2 * xh + xl, e] for xl in range(2)]
            ws[:, pl.ds(pl.multiple_of(t * zrows, 128), zrows)] = 0.25 * lax.dot_general(
                proj[...], jnp.concatenate(rows, axis=0), (((1,), (1,)), ((), ())),
                preferred_element_type=F32,
            )
        ws_copy(i).start()
        return carry

    lax.fori_loop(0, nz // 2, ws_step, 0)

    def ws_wait(i, carry):
        ws_copy(i).wait()
        return carry

    lax.fori_loop(0, nz // 2, ws_wait, 0)
    for copy in copies:
        copy.wait()


def on_device(nz, attn, cot, w, proj, m1, m2, steps):
    unit, rank = m1.shape
    tokens, inner = attn.shape
    width = cot.shape[1]
    rows = 4 * unit
    ne = nz // NY
    span = w.shape[0]
    q = span // 4
    dma = pltpu.SemaphoreType.DMA
    one = pltpu.SemaphoreType.DMA
    vm = pltpu.VMEM
    any_ = pl.BlockSpec(memory_space=pl.ANY)
    results = pl.pallas_call(
        functools.partial(kernel, nz, unit),
        out_shape=(
            vm((4, tokens, 2 * span), BF16),
            vm((2, 4, 4, ne, rows, rank), BF16),
            vm((span, rank), BF16),
            vm(m1.shape, F32),
            vm(m2.shape, F32),
        ),
        in_specs=[pl.BlockSpec(memory_space=pltpu.HBM)] * 6 + [pl.BlockSpec(memory_space=pltpu.SMEM)],
        out_specs=(pl.BlockSpec(memory_space=vm),) * 5,
        scratch_shapes=[
            vm((tokens, inner), BF16),
            vm((tokens, width), BF16),
            vm((8, 2, 2, q, width), BF16),
            vm((inner, rank), BF16),
            vm((tokens, rank), BF16),
            vm((nz, 2, 2 * rows, rank), F32),
            vm((nz, 2, 2 * rows, rank), BF16),
            vm((nz, 2, 2 * rows, rank), BF16),
            vm((4, 4, ne, rows, rank), BF16),
            vm((4, 4, ne, rows, rank), BF16),
            vm((4, ne, rows, rank), BF16),
            vm((4, ne, rows, rank), BF16),
            vm((ne, rows, rank), BF16),
            vm((nz, rows, rank), BF16),
            vm((NY, unit, rank), F32),
            vm((NY, unit, rank), F32),
            vm((NY, unit, rank), F32),
            vm((NY, unit, rank), F32),
            dma((5,)), dma((nz,)),
            one, dma((nz,)),
            one, one,
            one, one,
            dma((ne,)), one,
            dma((2,)), dma((2,)),
            dma((2,)), dma((2,)),
            one, dma((ne,)),
            one, dma((3,)),
            one, dma((3,)),
            one, one,
            one, dma((2,)),
            one, dma((2,)),
            one, dma((2,)),
            one, dma((8,)),
            one, dma((8,)),
            one, dma((8,)),
        ],
        compiler_params=pltpu.CompilerParams(
            collective_id=0, has_side_effects=True, vmem_limit_bytes=40 * 2**20
        ),
    )(
        *(
            pltpu.with_memory_space_constraint(a, pltpu.HBM)
            for a in (attn, cot, w.reshape(2, 2, q, width), proj, m1, m2)
        ),
        steps,
    )
    return pl.pallas_call(
        finish_kernel,
        out_shape=(
            jax.ShapeDtypeStruct((tokens, inner), BF16),
            jax.ShapeDtypeStruct((span, width), F32),
            jax.ShapeDtypeStruct(m1.shape, F32),
            jax.ShapeDtypeStruct(m2.shape, F32),
        ),
        in_specs=[pl.BlockSpec(memory_space=vm)] * 5,
        out_specs=(any_,) * 4,
        scratch_shapes=[vm((span, width), F32), dma((4,)), dma((nz // 2,)), dma((2,))],
        compiler_params=pltpu.CompilerParams(vmem_limit_bytes=16 * 2**20),
    )(*(pltpu.with_memory_space_constraint(a, vm) for a in results))


def solution(mesh):
    placed = (
        P(("dp", "fsdp"), None),
        P(("dp", "fsdp"), None),
        P("fsdp", None),
        P(),
        P(("dp", "fsdp"), None),
        P(("dp", "fsdp"), None),
        P(),
    )
    return jax.shard_map(
        functools.partial(on_device, mesh.shape["dp"] // 4),
        mesh=mesh,
        in_specs=placed,
        out_specs=(
            P(("dp", "fsdp"), None),
            P("fsdp", None),
            P(("dp", "fsdp"), None),
            P(("dp", "fsdp"), None),
        ),
        check_vma=False,
    )
```
